128 devices in a mesh: lon: 16 (over z_hi, y, core), lat: 8 (over z_lo, x).
Axes of the slice: x: 4, y: 4, z: 4 (z_hi: 2, z_lo: 2; z = z_hi * 2 + z_lo), core: 2. Of those that a mesh axis runs over, the one named last changes fastest.
Arguments:
- coarse: float32 [12, 64, 3072], P(None, 'lat', 'lon'), may hold values from -100 to 100
- static: float32 [4, 64, 3072], P(None, 'lat', 'lon'), may hold values from -16 to 16
- noise_seeds: int32 [64], replicated, may hold values from 0 to 1073741823
- regress_in: bfloat16 [3, 3, 16, 128], replicated, may hold values from -0.5 to 0.5
- regress_one: bfloat16 [3, 3, 128, 128], replicated, may hold values from -0.1875 to 0.1875
- regress_two: bfloat16 [3, 3, 128, 128], replicated, may hold values from -0.1875 to 0.1875
- regress_out: bfloat16 [3, 3, 128, 12], replicated, may hold values from -0.1875 to 0.1875
- diffuse_in: bfloat16 [3, 3, 40, 256], replicated, may hold values from -0.3125 to 0.3125
- diffuse_one: bfloat16 [3, 3, 256, 256], replicated, may hold values from -0.125 to 0.125
- diffuse_two: bfloat16 [3, 3, 256, 256], replicated, may hold values from -0.125 to 0.125
- diffuse_out: bfloat16 [3, 3, 256, 12], replicated, may hold values from -0.125 to 0.125
Outputs:
- mean_field: float32 [12, 64, 3072], P(None, 'lat', 'lon')
- field: float32 [12, 64, 3072], P(None, 'lat', 'lon')
The draws below stay inside these ranges and needn't reach their ends.
All inputs are finite; a program needn't handle non-finite values.
Results may differ from the reference program's by a relative error of at most 0.0034.
The reference program's roundings to bfloat16 on the way count: a program that leaves them out, or rounds other values in their place, can miss the bound.
Values may be sent and summed in bfloat16 or wider, within the bound.
A program may use at most 64 MiB of HBM per device.

```python
import jax
import jax.numpy as jnp
from jax import lax

LON_DEV = 192
MARGIN = 32
REG = 128
DIF = 256
OUTC = 12
INC = 12
STATIC = 4
GROUPS = 32
LAT_ALL = 64
LON_ALL = 3072
PATCH_W = 256
PATCHES = 16
IN_ALL = 16
DIF_IN = 40


def draw_coarse(key, part):
    key = jax.random.fold_in(key, 7)
    row_key, column_key, body_key = jax.random.split(key, 3)
    row_position = jnp.arange(LAT_ALL, dtype=jnp.float32) / LAT_ALL
    row_scale = jnp.exp(row_position * 1.0986123 + jax.random.uniform(row_key, (LAT_ALL,), jnp.float32, 0.0, 0.5))
    position = jnp.arange(LON_ALL, dtype=jnp.float32) / LON_ALL
    column_scale = jnp.exp(position * 1.0986123 + jax.random.uniform(column_key, (LON_ALL,), jnp.float32, 0.0, 0.5))
    base = jnp.clip(jax.random.normal(body_key, (INC, LAT_ALL, LON_ALL), jnp.float32), -4.0, 4.0)
    return base * row_scale[None, :, None] * column_scale[None, None, :]


def plant(values, own_key, low, top_value):
    shape = values.shape
    spot = [jax.random.randint(jax.random.fold_in(own_key, axis), (), 0, shape[axis]) for axis in range(len(shape))]
    values = values.at[tuple(spot)].set(low)
    longest = shape.index(max(shape))
    spot[longest] = (spot[longest] + 1) % shape[longest]
    return values.at[tuple(spot)].set(top_value)


def level_of(stream_key, extent, cuts, low, high):
    def one(axis_at, blocks):
        steps = jax.random.uniform(jax.random.fold_in(jax.random.fold_in(stream_key, 6), axis_at), (blocks,), jnp.float32, low / len(cuts), high / len(cuts))
        return jnp.repeat(jnp.exp(steps), extent[axis_at] // blocks).reshape((-1,) + (1,) * (len(extent) - axis_at - 1))

    factor_of = one(*cuts[0])
    for cut in cuts[1:]:
        factor_of = factor_of * one(*cut)
    return factor_of


def bell_draw(stream_key, shape, deviation, most, cuts=(), kind=jnp.bfloat16):
    result = deviation * jax.random.normal(stream_key, shape, jnp.float32)
    if cuts:
        result = result * level_of(stream_key, shape, cuts, -0.22, 0.18)
    return jnp.clip(result, -most, most).astype(kind)


def setup_inputs(seed: int = 0) -> dict:
    arg_keys = jax.random.split(jax.random.key(seed), 12)
    coarse = draw_coarse(jax.random.fold_in(arg_keys[11], 71), 0)
    static = bell_draw(arg_keys[1], (STATIC, LAT_ALL, LON_ALL), 3.0, 16.0, ((1, 8), (2, 16)), jnp.float32)
    noise_seeds = plant(jax.random.randint(arg_keys[2], (LAT_ALL,), 0, 1073741824), jax.random.fold_in(arg_keys[2], 1), 0, 1073741823).astype(jnp.int32)
    regress_in = bell_draw(arg_keys[3], (3, 3, IN_ALL, REG), (9 * IN_ALL) ** -0.5, 0.5)
    regress_one = bell_draw(arg_keys[4], (3, 3, REG, REG), (9 * REG) ** -0.5, 0.1875)
    regress_two = bell_draw(arg_keys[5], (3, 3, REG, REG), (9 * REG) ** -0.5, 0.1875)
    regress_out = bell_draw(arg_keys[6], (3, 3, REG, OUTC), (9 * REG) ** -0.5, 0.1875)
    diffuse_in = bell_draw(arg_keys[7], (3, 3, DIF_IN, DIF), (9 * DIF_IN) ** -0.5, 0.3125)
    diffuse_one = bell_draw(arg_keys[8], (3, 3, DIF, DIF), (9 * DIF) ** -0.5, 0.125)
    diffuse_two = bell_draw(arg_keys[9], (3, 3, DIF, DIF), (9 * DIF) ** -0.5, 0.125)
    diffuse_out = bell_draw(arg_keys[10], (3, 3, DIF, OUTC), (9 * DIF) ** -0.5, 0.125)
    return {"coarse": coarse, "static": static, "noise_seeds": noise_seeds, "regress_in": regress_in, "regress_one": regress_one, "regress_two": regress_two, "regress_out": regress_out, "diffuse_in": diffuse_in, "diffuse_one": diffuse_one, "diffuse_two": diffuse_two, "diffuse_out": diffuse_out}


EPSILON = 1e-05

def noise_hash(value):
    value = value ^ value >> 16 & 65535
    value = value * 73244475
    value = value ^ value >> 16 & 65535
    value = value * 73244475
    value = value ^ value >> 16 & 65535
    return value

def latent(row_seeds, column_ids, channels):
    channel_ids = jnp.arange(channels, dtype=jnp.int32)
    code = (column_ids.astype(jnp.int32)[None, None, :] * channels + channel_ids[:, None, None]) * 1640531527
    start = row_seeds.astype(jnp.int32)[None, :, None] ^ code
    total = jnp.zeros(start.shape, jnp.float32)
    for turn in range(4):
        mixed = noise_hash(start + turn * 374761393)
        total = total + ((mixed & 65535).astype(jnp.float32) * (1.0 / 65536.0) + 1.0 / 131072.0)
    return (total - 2.0) * 1.7320508075688772

def conv_valid(padded, weight):
    height = padded.shape[0] - 2
    width = padded.shape[1] - 2
    depth = padded.shape[2]
    total = jnp.zeros((height * width, weight.shape[3]), jnp.float32)
    for shift_row in range(3):
        for shift_column in range(3):
            piece = padded[shift_row:shift_row + height, shift_column:shift_column + width].reshape(height * width, depth)
            total = total + jnp.dot(piece, weight[shift_row, shift_column], preferred_element_type=jnp.float32)
    return total.reshape(height, width, weight.shape[3])

def group_stats(values, groups):
    channels = values.shape[-1]
    grouped = values.reshape(-1, groups, channels // groups)
    return (lax.optimization_barrier(jnp.sum(grouped, axis=(0, 2))), lax.optimization_barrier(jnp.sum(grouped * grouped, axis=(0, 2))))

def group_activate(values, sums, squares, cell_count, groups):
    channels = values.shape[-1]
    average = sums / cell_count
    variance = squares / cell_count - average * average
    scale = lax.rsqrt(variance + EPSILON)
    grouped = values.reshape(values.shape[:-1] + (groups, channels // groups))
    normed = (grouped - average[:, None]) * scale[:, None]
    return jax.nn.silu(normed).reshape(values.shape)

def pad_patch(values):
    return jnp.pad(values, ((1, 1), (1, 1), (0, 0)))

def pad_band(values):
    wrapped = jnp.concatenate([values[:, -1:], values, values[:, :1]], axis=1)
    return jnp.pad(wrapped, ((1, 1), (0, 0), (0, 0)))

def denoise(patch, diffuse_in, diffuse_one, diffuse_two, diffuse_out):
    cell_count = patch.shape[0] * patch.shape[1] * (diffuse_in.shape[3] // GROUPS)
    first = lax.optimization_barrier(conv_valid(pad_patch(patch), diffuse_in).astype(jnp.bfloat16))
    sums, squares = group_stats(first.astype(jnp.float32), GROUPS)
    active = group_activate(first.astype(jnp.float32), sums, squares, cell_count, GROUPS).astype(jnp.bfloat16)
    second = lax.optimization_barrier(conv_valid(pad_patch(active), diffuse_one).astype(jnp.bfloat16))
    sums, squares = group_stats(second.astype(jnp.float32), GROUPS)
    active = group_activate(second.astype(jnp.float32), sums, squares, cell_count, GROUPS).astype(jnp.bfloat16)
    third = (first.astype(jnp.float32) + conv_valid(pad_patch(active), diffuse_two)).astype(jnp.bfloat16)
    return conv_valid(pad_patch(third), diffuse_out)

def reference(coarse, static, noise_seeds, regress_in, regress_one, regress_two, regress_out, diffuse_in, diffuse_one, diffuse_two, diffuse_out):
    inputs = jnp.concatenate([coarse, static], axis=0).astype(jnp.bfloat16)
    image = jnp.transpose(inputs, (1, 2, 0))
    cell_count = LAT_ALL * LON_ALL * (REG // GROUPS)
    first = lax.optimization_barrier(conv_valid(pad_band(image), regress_in).astype(jnp.bfloat16))
    sums, squares = group_stats(first.astype(jnp.float32), GROUPS)
    active = group_activate(first.astype(jnp.float32), sums, squares, cell_count, GROUPS).astype(jnp.bfloat16)
    second = lax.optimization_barrier(conv_valid(pad_band(active), regress_one).astype(jnp.bfloat16))
    sums, squares = group_stats(second.astype(jnp.float32), GROUPS)
    active = group_activate(second.astype(jnp.float32), sums, squares, cell_count, GROUPS).astype(jnp.bfloat16)
    third = (first.astype(jnp.float32) + conv_valid(pad_band(active), regress_two)).astype(jnp.bfloat16)
    mean_field = jnp.transpose(conv_valid(pad_band(third), regress_out), (2, 0, 1))
    noise = latent(noise_seeds, jnp.arange(LON_ALL, dtype=jnp.int32), OUTC)
    joined = jnp.concatenate([noise.astype(jnp.bfloat16), mean_field.astype(jnp.bfloat16), inputs], axis=0)

    def one_patch(index):
        columns = (index * LON_DEV - MARGIN + jnp.arange(PATCH_W, dtype=jnp.int32)) % LON_ALL
        patch = jnp.transpose(jnp.take(joined, columns, axis=2), (1, 2, 0))
        return jnp.transpose(denoise(patch, diffuse_in, diffuse_one, diffuse_two, diffuse_out), (2, 0, 1))
    patches = lax.map(one_patch, jnp.arange(PATCHES, dtype=jnp.int32))
    centre = patches[..., MARGIN:MARGIN + LON_DEV]
    from_left = jnp.roll(patches[..., LON_DEV + MARGIN:], 1, axis=0)
    from_right = jnp.roll(patches[..., :MARGIN], -1, axis=0)
    middle = jnp.zeros(centre.shape[:-1] + (LON_DEV - 2 * MARGIN,), jnp.float32)
    summed = centre + jnp.concatenate([from_left, middle, from_right], axis=-1)
    weights = jnp.concatenate([jnp.full((MARGIN,), 2.0, jnp.float32), jnp.ones((LON_DEV - 2 * MARGIN,), jnp.float32), jnp.full((MARGIN,), 2.0, jnp.float32)])
    velocity = jnp.transpose(summed / weights, (1, 2, 0, 3)).reshape(OUTC, LAT_ALL, LON_ALL)
    field = mean_field + noise + velocity
    return (mean_field, field)
```

```python
import functools

import jax
import jax.numpy as jnp
from jax import lax
from jax.experimental import pallas as pl
from jax.experimental.pallas import tpu as pltpu
from jax.sharding import PartitionSpec as P

MESH = pl.DeviceIdType.MESH
F32 = jnp.float32
BF16 = jnp.bfloat16

LON, LAT = 16, 8
ALL = LON * LAT
ROWS = 8
COLS = 192
BAND_ROWS = ROWS * LAT
BAND_COLS = COLS * LON
MARGIN = 32
PATCH = COLS + 2 * MARGIN
SIDE = 40
W = COLS + 2 * SIDE
OFF = SIDE - MARGIN
FRAME = 3 * ROWS
CH = 16
REG = 128
DIF = 256
OUTC = 12
EPS = 1e-05

AROUND = ((0, -1), (0, 1), (-1, -1), (-1, 0), (-1, 1), (1, -1), (1, 0), (1, 1))


def hashed(value):
    for _ in range(2):
        value = value ^ (lax.shift_right_logical(value, 16))
        value = value * 73244475
    return value ^ (lax.shift_right_logical(value, 16))


def at_row(row, width):
    return pl.multiple_of(row * width, 16)


def all_groups(stats, size):
    lane = lax.broadcasted_iota(jnp.int32, stats.shape, 1)
    step = 1
    while step < size:
        up = pltpu.roll(stats, 128 - step, axis=1)
        down = pltpu.roll(stats, step, axis=1)
        stats = stats + jnp.where((lane // step) % 2 == 0, up, down)
        step *= 2
    return stats


def scale_shift(sums, squares, count):
    mean = sums / count
    scale = lax.rsqrt(squares / count - mean * mean + EPS)
    return 0.5 * scale, -0.5 * scale * mean


def half_silu(half):
    return half + half * jnp.tanh(half)


def fold(values):
    return jnp.sum(values.reshape(values.shape[0] // 8, 8, values.shape[1]), axis=0)


def kernel(
    coarse,
    static,
    seeds,
    w_in,
    w_one_hbm,
    w_two_hbm,
    w_out,
    d_in,
    d_one_hbm,
    d_two_hbm,
    d_out,
    mean_out,
    field_out,
    w_one,
    w_two,
    d_one,
    d_two,
    own32,
    own16,
    tall,
    wide,
    xw,
    wb_in,
    wb_patch,
    wb_mean,
    wb_vel,
    first,
    second,
    third,
    act,
    noise_keep,
    parts,
    partial,
    mean_acc,
    p_first,
    p_second,
    p_third,
    p_act,
    pad32,
    edge_send,
    edge_recv,
    stat_send,
    stat_one,
    stat_two,
    stat_three,
    stat_four,
    w_sem,
    in_send,
    in_recv,
    st_send,
    st_recv,
    e_send,
    e_recv,
):
    lon = lax.axis_index("lon")
    lat = lax.axis_index("lat")
    me = lon * LAT + lat

    def partner(step):
        other = lax.rem(me + step, ALL)
        return {"lon": other // LAT, "lat": lax.rem(other, LAT)}

    def row_ok(e):
        row = lat * ROWS - ROWS + e
        return jnp.where((row >= 0) & (row < BAND_ROWS), 1.0, 0.0).astype(F32)

    loads = [
        pltpu.make_async_copy(src, dst, w_sem.at[i])
        for i, (src, dst) in enumerate(
            ((w_one_hbm, w_one), (w_two_hbm, w_two), (d_one_hbm, d_one), (d_two_hbm, d_two))
        )
    ]
    for load in loads:
        load.start()
    barrier = pltpu.get_barrier_semaphore()

    def greet(step, carry):
        pl.semaphore_signal(barrier, inc=1, device_id=partner(step), device_id_type=MESH)
        return carry

    lax.fori_loop(1, ALL, greet, 0)

    own32[...] = jnp.zeros_like(own32)
    for r in range(ROWS):
        own32[r * CH : r * CH + 12, 0:COLS] = coarse[:, r, :]
        own32[r * CH + 12 : r * CH + 16, 0:COLS] = static[:, r, :]
    own16[...] = own32[...].astype(BF16)

    wb_in[...] = jnp.zeros_like(wb_in)
    for p in range(6):
        for dy in range(3):
            for dx in range(3):
                at = dx * 128 + (p + dy) * CH
                wb_in[at : at + CH, p * REG : (p + 1) * REG] = w_in[dy * 3 + dx]
    wb_patch[...] = jnp.zeros_like(wb_patch)
    low_rows = lax.broadcasted_iota(jnp.int32, (40, DIF), 0) < OUTC
    for dy in range(3):
        for dx in range(3):
            raw = d_in[dy * 3 + dx].astype(F32)
            pieces = (
                jnp.where(low_rows, raw, 0.0)[:CH].astype(BF16),
                raw[24:40].astype(BF16),
                jnp.where(low_rows, pltpu.roll(raw, 28, axis=0), 0.0)[:CH].astype(BF16),
            )
            for part, piece in enumerate(pieces):
                for p in range(6):
                    at = part * 384 + dx * 128 + (p + dy) * CH
                    wb_patch[at : at + CH, p * DIF : (p + 1) * DIF] = piece
    pad32[...] = jnp.zeros_like(pad32)
    lane256 = lax.broadcasted_iota(jnp.int32, (1, 256), 1)
    lane128 = lax.broadcasted_iota(jnp.int32, (1, 128), 1)
    for dx in range(3):
        base = jnp.zeros((REG, 128), F32)
        for dy in range(3):
            pad32[0:REG, 0:OUTC] = w_out[dy * 3 + dx].astype(F32)
            base = base + pltpu.roll(pad32[0:REG, :], (2 - dy) * CH, axis=1)
        base = jnp.concatenate([base, jnp.zeros((REG, 128), F32)], axis=1)
        for e in range(3, 21):
            moved = pltpu.roll(base, ((e - 5) * CH) % 256, axis=1)
            if e < 5:
                moved = jnp.where(lane256 < (e - 2) * CH, moved, 0.0)
            if e > 18:
                moved = jnp.where(lane256 >= (e - 5) * CH, moved, 0.0)
            wb_mean[(e - 3) * REG : (e - 2) * REG, dx * 256 : (dx + 1) * 256] = moved.astype(BF16)
    for dx in range(3):
        base = jnp.zeros((DIF, 128), F32)
        for dy in range(3):
            pad32[:, 0:OUTC] = d_out[dy * 3 + dx].astype(F32)
            base = base + pltpu.roll(pad32[...], (2 - dy) * CH, axis=1)
        for e in range(7, 17):
            moved = pltpu.roll(base, ((e - 9) * CH) % 128, axis=1)
            if e < 9:
                moved = jnp.where(lane128 < (e - 6) * CH, moved, 0.0)
            if e > 14:
                moved = jnp.where(lane128 >= (e - 9) * CH, moved, 0.0)
            wb_vel[(e - 7) * DIF : (e - 6) * DIF, dx * 128 : (dx + 1) * 128] = moved.astype(BF16)

    lane_row = lane256 // CH
    lane_ok = jnp.zeros((1, 256), F32)
    seed = jnp.zeros((1, 256), jnp.int32)
    for r in range(16):
        row = lat * ROWS - 4 + r
        here = seeds[jnp.clip(row, 0, BAND_ROWS - 1)]
        seed = jnp.where(lane_row == r, here, seed)
        lane_ok = jnp.where(lane_row == r, row_ok(4 + r), lane_ok)

    def shift(values, dx):
        count = values.shape[0]
        spot = lax.broadcasted_iota(jnp.int32, values.shape, 0)
        if dx == 0:
            return jnp.where(spot == 0, 0.0, pltpu.roll(values, 1, axis=0))
        if dx == 2:
            return jnp.where(spot == count - 1, 0.0, pltpu.roll(values, count - 1, axis=0))
        return values

    def put_part(part, values):
        for dx in range(3):
            moved = shift(values, dx)
            at = part * 384 + dx * 128
            parts[0, :, at : at + 128] = moved[:, :128].astype(BF16)
            parts[1, :, at : at + 128] = pltpu.roll(moved, 192, axis=1)[:, :128].astype(BF16)
            parts[2, :, at : at + 128] = moved[:, 128:].astype(BF16)

    def noise_rows(i, carry):
        at = pl.multiple_of(i * 32, 32)
        column = lon * COLS - MARGIN + at + lax.broadcasted_iota(jnp.int32, (32, 256), 0)
        column = jnp.where(column < 0, column + BAND_COLS, column)
        column = jnp.where(column >= BAND_COLS, column - BAND_COLS, column)
        channel = lax.broadcasted_iota(jnp.int32, (32, 256), 1) % CH
        start = seed ^ ((column * OUTC + channel) * 1640531527)
        total = jnp.zeros((32, 256), jnp.int32)
        for turn in range(4):
            total = total + (hashed(start + turn * 374761393) & 65535)
        uniform = total.astype(F32) * (1.0 / 65536.0) + 4.0 / 131072.0
        noise_keep[pl.ds(at, 32), :] = (uniform - 2.0) * 1.7320508075688772 * lane_ok
        return carry

    lax.fori_loop(0, PATCH // 32, noise_rows, 0)
    put_part(0, noise_keep[...])

    pl.semaphore_wait(barrier, ALL - 1)

    def around(k):
        dlon, dlat = AROUND[k]
        target = {"lon": lax.rem(lon + dlon + LON, LON), "lat": lax.rem(lat + dlat + LAT, LAT)}
        if dlon == 0:
            src, dst = own16, tall.at[k]
        elif dlon == 1:
            src, dst = own16.at[:, 128:256], wide.at[k - 2]
        else:
            src, dst = own16.at[:, 0:128], wide.at[k - 2]
        return pltpu.make_async_remote_copy(
            src_ref=src,
            dst_ref=dst,
            send_sem=in_send.at[k],
            recv_sem=in_recv.at[k],
            device_id=target,
            device_id_type=MESH,
        )

    order = (2, 4, 5, 7, 3, 6, 0, 1)
    copies = {k: around(k) for k in order}
    for k in order:
        copies[k].start()
    for k in order:
        copies[k].wait_recv()

    def assemble(centre, left, right):
        lane = lax.broadcasted_iota(jnp.int32, (128, 384), 1)
        zeros = jnp.zeros((128, 128), F32)
        mid = pltpu.roll(jnp.concatenate([centre, zeros], axis=1), SIDE, axis=1)
        low = pltpu.roll(jnp.concatenate([left, zeros, zeros], axis=1), 384 - 24, axis=1)
        high = pltpu.roll(jnp.concatenate([right, zeros, zeros], axis=1), SIDE + COLS, axis=1)
        inner = jnp.where(lane < SIDE + COLS, mid, jnp.where(lane < W, high, 0.0))
        return jnp.where(lane < SIDE, low, inner)

    up = assemble(tall[1].astype(F32), wide[7 - 2].astype(F32), wide[4 - 2].astype(F32))
    mid = assemble(own16[...].astype(F32), wide[6 - 2].astype(F32), wide[3 - 2].astype(F32))
    down = assemble(tall[0].astype(F32), wide[5 - 2].astype(F32), wide[2 - 2].astype(F32))
    up = jnp.where(lat == 0, 0.0, up)
    down = jnp.where(lat == LAT - 1, 0.0, down)
    xt = jnp.concatenate([up.T, mid.T, down.T], axis=1)[:W]
    xt_far = pltpu.roll(xt, 320, axis=1)
    for dx in range(3):
        if dx == 0:
            near, far = pltpu.roll(xt, 1, axis=0), pltpu.roll(xt_far, 1, axis=0)
        elif dx == 2:
            near, far = pltpu.roll(xt, W - 1, axis=0), pltpu.roll(xt_far, W - 1, axis=0)
        else:
            near, far = xt, xt_far
        for win in range(5):
            source = (near, far)[win % 2]
            at = (win // 2) * 128
            xw[win, :, dx * 128 : (dx + 1) * 128] = source[:, at : at + 128].astype(BF16)

    def first_rows(win, low, high):
        out = jnp.dot(
            xw[win], wb_in[:, low * REG : high * REG], preferred_element_type=F32
        ).astype(BF16)
        s = jnp.zeros((8, REG), F32)
        q = jnp.zeros((8, REG), F32)
        for p in range(low, high):
            e = win * 4 + 1 + p
            row = out[:, (p - low) * REG : (p - low + 1) * REG]
            first[e * W : (e + 1) * W, :] = row
            if 8 <= e < 16:
                cell = row[SIDE : SIDE + COLS].astype(F32)
                s = s + fold(cell)
                q = q + fold(cell * cell)
        return s, q

    def send_band(which, s, q, recv):
        stat_send[which, 0:1, :] = jnp.sum(s, axis=0, keepdims=True)
        stat_send[which, 1:2, :] = jnp.sum(q, axis=0, keepdims=True)

        def one(step, carry):
            pltpu.make_async_remote_copy(
                src_ref=stat_send.at[which, pl.ds(0, 2)],
                dst_ref=recv.at[step - 1],
                send_sem=st_send.at[which],
                recv_sem=st_recv.at[which],
                device_id=partner(step),
                device_id_type=MESH,
            ).start()
            return carry

        lax.fori_loop(1, ALL, one, 0)

    def band_scale(which, recv):
        pltpu.make_async_copy(recv, recv, st_recv.at[which]).wait()
        stat_send[4 + which, 0:2, :] = stat_send[which, 0:2, :] + jnp.sum(recv[...], axis=0)
        total = all_groups(stat_send[4 + which], REG // 32)
        return scale_shift(
            total[0:1], total[1:2], float(BAND_ROWS * BAND_COLS * (REG // 32))
        )

    def send_patch(which, s, q, recv):
        s = jnp.sum(s, axis=0, keepdims=True)
        q = jnp.sum(q, axis=0, keepdims=True)
        stat_send[which, 0:1, :] = s[:, :128]
        stat_send[which, 1:2, :] = s[:, 128:]
        stat_send[which, 2:3, :] = q[:, :128]
        stat_send[which, 3:4, :] = q[:, 128:]
        for step in range(1, LAT):
            pltpu.make_async_remote_copy(
                src_ref=stat_send.at[which, pl.ds(0, 4)],
                dst_ref=recv.at[step - 1],
                send_sem=st_send.at[which],
                recv_sem=st_recv.at[which],
                device_id={"lat": lax.rem(lat + step, LAT)},
                device_id_type=MESH,
            ).start()

    def patch_scale(which, recv):
        pltpu.make_async_copy(recv, recv, st_recv.at[which]).wait()
        stat_send[4 + which, 0:4, :] = stat_send[which, 0:4, :] + jnp.sum(recv[...], axis=0)
        total = all_groups(stat_send[4 + which], DIF // 32)
        sums = jnp.concatenate([total[0:1], total[1:2]], axis=1)
        squares = jnp.concatenate([total[2:3], total[3:4]], axis=1)
        return scale_shift(sums, squares, float(BAND_ROWS * PATCH * (DIF // 32)))

    stats = [first_rows(1, 3, 6), first_rows(2, 2, 4), first_rows(3, 0, 3)]
    stat_send[...] = jnp.zeros_like(stat_send)
    send_band(0, sum(s for s, _ in stats), sum(q for _, q in stats), stat_one)

    first_rows(0, 0, 6)
    first_rows(1, 2, 3)
    first_rows(3, 3, 6)
    first_rows(4, 2, 6)
    own_xt = xt_far[OFF : OFF + PATCH, :256]
    put_part(1, own_xt)

    def patch_rows(win):
        return ((3, 6), (2, 4), (0, 3))[win]

    def rest_rows(win):
        return ((0, 3), None, (3, 6))[win]

    for win in range(3):
        for span in (patch_rows(win), rest_rows(win)):
            if span is None:
                continue
            low, high = span
            out = jnp.dot(
                parts[win, :, 0:768],
                wb_patch[0:768, low * DIF : high * DIF],
                preferred_element_type=F32,
            )
            for p in range(low, high):
                e = win * 4 + 5 + p
                partial[(e - 5) * PATCH : (e - 4) * PATCH, :] = out[
                    :, (p - low) * DIF : (p - low + 1) * DIF
                ]

    def activate_band(source, a, b, e):
        ok = row_ok(e)
        at = at_row(e, W)
        half = source[pl.ds(at, W), :].astype(F32) * (a * ok) + b * ok
        out = half_silu(half)
        act[0, pl.ds(at, W), :] = pltpu.roll(out, 1, axis=0).astype(BF16)
        act[1, pl.ds(at, W), :] = out.astype(BF16)
        act[2, pl.ds(at, W), :] = pltpu.roll(out, W - 1, axis=0).astype(BF16)

    def loop(count, body):
        lax.fori_loop(0, count, lambda i, c: (body(i), c)[1], 0)

    def conv_band(weight, e, rows):
        lhs = jnp.concatenate(
            [
                act[dx, pl.ds(at_row(e + dy - 1, W), rows * W), :]
                for dy in range(3)
                for dx in range(3)
            ],
            axis=1,
        )
        return jnp.dot(lhs, weight[...], preferred_element_type=F32)

    a, b = band_scale(0, stat_one)
    loop(10, lambda i: activate_band(first, a, b, i + 7))
    loads[0].wait()

    def second_own(i, carry):
        s, q = carry
        e = 8 + i
        out = conv_band(w_one, e, 1).astype(BF16)
        second[pl.ds(at_row(e, W), W), :] = out
        cell = out[SIDE : SIDE + COLS].astype(F32)
        return s + fold(cell), q + fold(cell * cell)

    zero = jnp.zeros((8, REG), F32)
    s, q = lax.fori_loop(0, ROWS, second_own, (zero, zero))
    send_band(1, s, q, stat_two)

    def second_rest(i):
        e = 2 + i + (i // 6) * 8
        second[pl.ds(at_row(e, W), W), :] = conv_band(w_one, e, 1).astype(BF16)

    loop(12, lambda i: activate_band(first, a, b, 1 + i + (i // 6) * 10))
    loop(12, second_rest)

    a2, b2 = band_scale(1, stat_two)
    loop(14, lambda i: activate_band(second, a2, b2, i + 5))
    loads[1].wait()

    def third_row(e):
        at = at_row(e, W)
        out = first[pl.ds(at, W), :].astype(F32) + conv_band(w_two, e, 1)
        third[pl.ds(at, W), :] = (out * row_ok(e)).astype(BF16)

    loop(12, lambda i: third_row(i + 6))

    def mean_terms(low, high):
        lhs = jnp.concatenate([third[e * W : (e + 1) * W, :] for e in range(low, high)], axis=1)
        return [
            jnp.dot(
                lhs,
                wb_mean[(low - 3) * REG : (high - 3) * REG, dx * 256 : (dx + 1) * 256],
                preferred_element_type=F32,
            )
            for dx in range(3)
        ]

    def put_mean():
        total = (
            pltpu.roll(mean_acc[0], 1, axis=0)
            + mean_acc[1]
            + pltpu.roll(mean_acc[2], W - 1, axis=0)
        )[OFF : OFF + PATCH]
        put_part(2, total * lane_ok)
        return total

    def patch_first_rows(win, span):
        low, high = span
        out = jnp.dot(
            parts[win, :, 768:1152],
            wb_patch[768:1152, low * DIF : high * DIF],
            preferred_element_type=F32,
        )
        s = jnp.zeros((8, DIF), F32)
        q = jnp.zeros((8, DIF), F32)
        for p in range(low, high):
            e = win * 4 + 5 + p
            at = (e - 5) * PATCH
            row = out[:, (p - low) * DIF : (p - low + 1) * DIF] + partial[at : at + PATCH, :]
            row = row.astype(BF16)
            p_first[at : at + PATCH, :] = row
            if 8 <= e < 16:
                cell = row.astype(F32)
                s = s + fold(cell)
                q = q + fold(cell * cell)
        return s, q

    for dx, term in enumerate(mean_terms(6, 18)):
        mean_acc[dx] = term
    put_mean()
    stats = [patch_first_rows(win, patch_rows(win)) for win in range(3)]
    send_patch(2, sum(s for s, _ in stats), sum(q for _, q in stats), stat_three)

    def activate_rest(i):
        activate_band(second, a2, b2, 2 + i + (i // 3) * 14)

    loop(6, activate_rest)
    loop(6, lambda i: third_row(3 + i + (i // 3) * 12))
    for low, high in ((3, 6), (18, 21)):
        for dx, term in enumerate(mean_terms(low, high)):
            mean_acc[dx] = mean_acc[dx] + term
    mean_all = put_mean()
    mean_own = pltpu.roll(mean_all, 192, axis=1)[:, :128]
    noise_own = pltpu.roll(noise_keep[...], 192, axis=1)[:, :128]
    base = mean_own + noise_own

    def put_out(out_ref, values):
        flat = pltpu.roll(values.T, PATCH - MARGIN, axis=1)[:, :COLS]
        for r in range(ROWS):
            out_ref[:, r, :] = flat[r * CH : r * CH + OUTC, :]

    put_out(mean_out, mean_own)
    pad32[...] = base
    patch_first_rows(0, rest_rows(0))
    patch_first_rows(2, rest_rows(2))

    def activate_patch(source, shift_row, a, b, e):
        ok = row_ok(e)
        half = source[pl.ds(at_row(e - shift_row, PATCH), PATCH), :].astype(F32) * (a * ok) + b * ok
        out = half_silu(half)
        at = at_row(e - 5, PATCH)
        for dx in range(3):
            p_act[dx, pl.ds(at, PATCH), :] = shift(out, dx).astype(BF16)

    def conv_patch(weight, e):
        lhs = jnp.concatenate(
            [
                p_act[dx, pl.ds(at_row(e + dy - 6, PATCH), PATCH), :]
                for dy in range(3)
                for dx in range(3)
            ],
            axis=1,
        )
        return jnp.dot(lhs, weight[...], preferred_element_type=F32)

    a3, b3 = patch_scale(2, stat_three)
    loop(10, lambda i: activate_patch(p_first, 5, a3, b3, i + 7))
    loads[2].wait()

    def p_second_own(i, carry):
        s, q = carry
        e = 8 + i
        out = conv_patch(d_one, e).astype(BF16)
        p_second[pl.ds(at_row(e - 6, PATCH), PATCH), :] = out
        cell = out.astype(F32)
        return s + fold(cell), q + fold(cell * cell)

    zero = jnp.zeros((8, DIF), F32)
    s, q = lax.fori_loop(0, ROWS, p_second_own, (zero, zero))
    send_patch(3, s, q, stat_four)

    def p_second_rest(i):
        e = 6 + i + (i // 2) * 8
        p_second[pl.ds(at_row(e - 6, PATCH), PATCH), :] = conv_patch(d_one, e).astype(BF16)

    loop(4, lambda i: activate_patch(p_first, 5, a3, b3, 5 + i + (i // 2) * 10))
    loop(4, p_second_rest)

    a4, b4 = patch_scale(3, stat_four)
    loop(12, lambda i: activate_patch(p_second, 6, a4, b4, i + 6))
    loads[3].wait()

    def p_third_row(i):
        e = 7 + i
        out = p_first[pl.ds(at_row(e - 5, PATCH), PATCH), :].astype(F32) + conv_patch(d_two, e)
        p_third[pl.ds(at_row(e - 7, PATCH), PATCH), :] = (out * row_ok(e)).astype(BF16)

    loop(10, p_third_row)

    lhs = jnp.concatenate([p_third[e * PATCH : (e + 1) * PATCH, :] for e in range(10)], axis=1)
    out = jnp.dot(lhs, wb_vel[...], preferred_element_type=F32)
    velocity = shift(out[:, 0:128], 0) + out[:, 128:256] + shift(out[:, 256:384], 2)
    edge_send[0] = velocity[0:MARGIN]
    edge_send[1] = velocity[PATCH - MARGIN : PATCH]
    edges = [
        pltpu.make_async_remote_copy(
            src_ref=edge_send.at[k],
            dst_ref=edge_recv.at[k],
            send_sem=e_send.at[k],
            recv_sem=e_recv.at[k],
            device_id={"lon": lax.rem(lon + LON + step, LON)},
            device_id_type=MESH,
        )
        for k, step in ((0, -1), (1, 1))
    ]
    for edge in edges:
        edge.start()
    for k in order:
        copies[k].wait_send()
    for which, recv in enumerate((stat_one, stat_two, stat_three, stat_four)):
        pltpu.make_async_copy(recv, recv, st_send.at[which]).wait()
    for edge in edges:
        edge.wait()
    from_left = velocity[MARGIN : 2 * MARGIN] + edge_recv[1]
    from_right = velocity[COLS : COLS + MARGIN] + edge_recv[0]
    total = jnp.concatenate(
        [
            velocity[0:MARGIN],
            from_left * 0.5,
            velocity[2 * MARGIN : COLS],
            from_right * 0.5,
            velocity[COLS + MARGIN :],
        ],
        axis=0,
    )
    put_out(field_out, pad32[...] + total)


def on_device(coarse, static, noise_seeds, w_in, w_one, w_two, w_out, d_in, d_one, d_two, d_out):
    vmem = pl.BlockSpec(memory_space=pltpu.VMEM)
    smem = pl.BlockSpec(memory_space=pltpu.SMEM)
    hbm = pl.BlockSpec(memory_space=pl.ANY)
    out = jax.ShapeDtypeStruct((OUTC, ROWS, COLS), F32)
    return pl.pallas_call(
        kernel,
        out_shape=(out, out),
        in_specs=[vmem, vmem, smem, vmem, hbm, hbm, vmem, vmem, hbm, hbm, vmem],
        out_specs=(vmem, vmem),
        scratch_shapes=[
            pltpu.VMEM((9 * REG, REG), BF16),
            pltpu.VMEM((9 * REG, REG), BF16),
            pltpu.VMEM((9 * DIF, DIF), BF16),
            pltpu.VMEM((9 * DIF, DIF), BF16),
            pltpu.VMEM((128, 256), F32),
            pltpu.VMEM((128, 256), BF16),
            pltpu.VMEM((2, 128, 256), BF16),
            pltpu.VMEM((6, 128, 128), BF16),
            pltpu.VMEM((5, W, 384), BF16),
            pltpu.VMEM((384, 6 * REG), BF16),
            pltpu.VMEM((1152, 6 * DIF), BF16),
            pltpu.VMEM((18 * REG, 768), BF16),
            pltpu.VMEM((10 * DIF, 384), BF16),
            pltpu.VMEM((FRAME * W, REG), BF16),
            pltpu.VMEM((FRAME * W, REG), BF16),
            pltpu.VMEM((FRAME * W, REG), BF16),
            pltpu.VMEM((3, FRAME * W, REG), BF16),
            pltpu.VMEM((PATCH, 256), F32),
            pltpu.VMEM((3, PATCH, 1152), BF16),
            pltpu.VMEM((14 * PATCH, DIF), F32),
            pltpu.VMEM((3, W, 256), F32),
            pltpu.VMEM((14 * PATCH, DIF), BF16),
            pltpu.VMEM((12 * PATCH, DIF), BF16),
            pltpu.VMEM((10 * PATCH, DIF), BF16),
            pltpu.VMEM((3, 14 * PATCH, DIF), BF16),
            pltpu.VMEM((256, 128), F32),
            pltpu.VMEM((2, MARGIN, 128), F32),
            pltpu.VMEM((2, MARGIN, 128), F32),
            pltpu.VMEM((8, 8, 128), F32),
            pltpu.VMEM((ALL - 1, 2, 128), F32),
            pltpu.VMEM((ALL - 1, 2, 128), F32),
            pltpu.VMEM((LAT - 1, 4, 128), F32),
            pltpu.VMEM((LAT - 1, 4, 128), F32),
            pltpu.SemaphoreType.DMA((4,)),
            pltpu.SemaphoreType.DMA((8,)),
            pltpu.SemaphoreType.DMA((8,)),
            pltpu.SemaphoreType.DMA((4,)),
            pltpu.SemaphoreType.DMA((4,)),
            pltpu.SemaphoreType.DMA((2,)),
            pltpu.SemaphoreType.DMA((2,)),
        ],
        compiler_params=pltpu.CompilerParams(
            collective_id=0, has_side_effects=True, vmem_limit_bytes=60 * 1024 * 1024
        ),
    )(
        coarse,
        static,
        noise_seeds,
        w_in.reshape(9, CH, REG),
        w_one.reshape(9 * REG, REG),
        w_two.reshape(9 * REG, REG),
        w_out.reshape(9, REG, OUTC),
        d_in.reshape(9, 40, DIF),
        d_one.reshape(9 * DIF, DIF),
        d_two.reshape(9 * DIF, DIF),
        d_out.reshape(9, DIF, OUTC),
    )


def solution(mesh):
    brick = P(None, "lat", "lon")
    return jax.shard_map(
        on_device,
        mesh=mesh,
        in_specs=(brick, brick) + (P(),) * 9,
        out_specs=(brick, brick),
        check_vma=False,
    )
```

```python
import functools

import jax
import jax.numpy as jnp
from jax import lax
from jax.experimental import pallas as pl
from jax.experimental.pallas import tpu as pltpu
from jax.sharding import PartitionSpec as P

MESH = pl.DeviceIdType.MESH
F32 = jnp.float32
BF16 = jnp.bfloat16

LON, LAT = 16, 8
ALL = LON * LAT
ROWS = 8
COLS = 192
BAND_ROWS = ROWS * LAT
BAND_COLS = COLS * LON
MARGIN = 32
PATCH = COLS + 2 * MARGIN
SIDE = 40
W = COLS + 2 * SIDE
OFF = SIDE - MARGIN
FRAME = 3 * ROWS
CH = 16
REG = 128
DIF = 256
OUTC = 12
STEPS = (2, 1, 3, 0)
EPS = 1e-05

AROUND = ((0, -1), (0, 1), (-1, -1), (-1, 0), (-1, 1), (1, -1), (1, 0), (1, 1))


def hashed(value):
    for _ in range(2):
        value = value ^ (lax.shift_right_logical(value, 16))
        value = value * 73244475
    return value ^ (lax.shift_right_logical(value, 16))


def at_row(row, width):
    return pl.multiple_of(row * width, 16)


def all_groups(stats, size):
    lane = lax.broadcasted_iota(jnp.int32, stats.shape, 1)
    step = 1
    while step < size:
        up = pltpu.roll(stats, 128 - step, axis=1)
        down = pltpu.roll(stats, step, axis=1)
        stats = stats + jnp.where((lane // step) % 2 == 0, up, down)
        step *= 2
    return stats


def scale_shift(sums, squares, count):
    mean = sums / count
    scale = lax.rsqrt(squares / count - mean * mean + EPS)
    return 0.5 * scale, -0.5 * scale * mean


def half_silu(half):
    return half + half * jnp.tanh(half)


def fold(values):
    return jnp.sum(values.reshape(values.shape[0] // 8, 8, values.shape[1]), axis=0)


def kernel(
    coarse_hbm,
    static_hbm,
    seeds,
    w_in,
    w_one_hbm,
    w_two_hbm,
    w_out,
    d_in,
    d_one_hbm,
    d_two_hbm,
    d_out,
    mean_out,
    field_out,
    coarse,
    static,
    w_one,
    w_two,
    d_one,
    d_two,
    own32,
    own16,
    tall,
    wide,
    xw,
    wb_in,
    wb_patch,
    wb_mean,
    wb_vel,
    first,
    second,
    third,
    act,
    noise_keep,
    parts,
    partial,
    mean_acc,
    p_first,
    p_second,
    p_third,
    p_act,
    pad32,
    taps,
    edge_send,
    edge_recv,
    stat_send,
    stat_one,
    stat_two,
    stat_three,
    stat_four,
    w_sem,
    in_send,
    in_recv,
    st_send,
    st_recv,
    e_send,
    e_recv,
):
    lon = lax.axis_index("lon")
    lat = lax.axis_index("lat")

    core = lax.rem(lon, 2)
    y = lax.rem(lon // 2, 4)
    x = lax.rem(lat, 4)
    z = (lon // 8) * 2 + lat // 4

    def chip(dz, dy, dx):
        there = lax.rem(z + dz, 4)
        far_lon = (there // 2) * 8 + lax.rem(y + dy, 4) * 2
        return far_lon, lax.rem(there, 2) * 4 + lax.rem(x + dx, 4)

    def reach(i):
        return jnp.where(i == 0, 2, jnp.where(i == 3, 0, jnp.where(i == 1, 1, 3)))

    def to_all(action):
        def some(i, carry):
            dz, dy = reach(i // 4), reach(lax.rem(i, 4))
            for j, dx in enumerate(STEPS):
                far_lon, far_lat = chip(dz, dy, dx)
                for k in range(2):
                    target = {"lon": far_lon + (1 - core if k == 0 else core), "lat": far_lat}
                    action(target, i * 8 + j * 2 + k)
            return carry

        lax.fori_loop(0, 15, some, 0)
        for j, dx in enumerate(STEPS):
            far_lon, far_lat = chip(0, 0, dx)
            for k in range(2):
                if (j, k) != (3, 1):
                    target = {"lon": far_lon + (1 - core if k == 0 else core), "lat": far_lat}
                    action(target, 120 + j * 2 + k)

    def row_ok(e):
        row = lat * ROWS - ROWS + e
        return jnp.where((row >= 0) & (row < BAND_ROWS), 1.0, 0.0).astype(F32)

    barrier = pltpu.get_barrier_semaphore()

    to_all(
        lambda target, slot: pl.semaphore_signal(
            barrier, inc=1, device_id=target, device_id_type=MESH
        )
    )

    wide_w = ((w_one_hbm, w_one), (w_two_hbm, w_two))
    loads = []
    for i, (src, dst) in enumerate(wide_w):
        dst[3 * 384 : 4 * 384, 0:128] = jnp.zeros((384, 128), BF16)
        dst[0:384, 128:256] = jnp.zeros((384, 128), BF16)
        loads.append(
            [
                pltpu.make_async_copy(
                    src,
                    dst.at[p * 384 : p * 384 + 9 * REG, p * 128 : (p + 1) * 128],
                    w_sem.at[i * 2 + p],
                )
                for p in range(2)
            ]
        )
    loads.append([pltpu.make_async_copy(d_one_hbm, d_one, w_sem.at[4])])
    loads.append([pltpu.make_async_copy(d_two_hbm, d_two, w_sem.at[5])])
    near = [
        pltpu.make_async_copy(coarse_hbm, coarse, w_sem.at[6]),
        pltpu.make_async_copy(static_hbm, static, w_sem.at[7]),
    ]
    for load in near:
        load.start()
    for group in loads:
        for load in group:
            load.start()
    for load in near:
        load.wait()
    own32[...] = jnp.zeros_like(own32)
    for r in range(ROWS):
        own32[r * CH : r * CH + 12, 0:COLS] = coarse[:, r, :]
        own32[r * CH + 12 : r * CH + 16, 0:COLS] = static[:, r, :]
    own16[...] = own32[...].astype(BF16)

    wb_in[...] = jnp.zeros_like(wb_in)
    for p in range(6):
        for dy in range(3):
            for dx in range(3):
                at = dx * 128 + (p + dy) * CH
                wb_in[at : at + CH, p * REG : (p + 1) * REG] = w_in[dy * 3 + dx]
    wb_patch[...] = jnp.zeros_like(wb_patch)
    low_rows = lax.broadcasted_iota(jnp.int32, (40, DIF), 0) < OUTC
    for dy in range(3):
        for dx in range(3):
            raw = d_in[dy * 3 + dx].astype(F32)
            pieces = (
                jnp.where(low_rows, raw, 0.0)[:CH].astype(BF16),
                raw[24:40].astype(BF16),
                jnp.where(low_rows, pltpu.roll(raw, 28, axis=0), 0.0)[:CH].astype(BF16),
            )
            for part, piece in enumerate(pieces):
                for p in range(6):
                    at = part * 384 + dx * 128 + (p + dy) * CH
                    wb_patch[at : at + CH, p * DIF : (p + 1) * DIF] = piece
    taps[...] = jnp.zeros_like(taps)
    lane256 = lax.broadcasted_iota(jnp.int32, (1, 256), 1)
    lane128 = lax.broadcasted_iota(jnp.int32, (1, 128), 1)
    for dx in range(3):
        for dy in range(3):
            taps[(2 - dy) * CH : (2 - dy) * CH + OUTC, 0:REG] = w_out[dy * 3 + dx].astype(F32)
        base = jnp.concatenate([taps[:, 0:REG].T, jnp.zeros((REG, 128), F32)], axis=1)
        for e in range(3, 21):
            moved = pltpu.roll(base, ((e - 5) * CH) % 256, axis=1)
            if e < 5:
                moved = jnp.where(lane256 < (e - 2) * CH, moved, 0.0)
            if e > 18:
                moved = jnp.where(lane256 >= (e - 5) * CH, moved, 0.0)
            wb_mean[(e - 3) * REG : (e - 2) * REG, dx * 256 : (dx + 1) * 256] = moved.astype(BF16)
    for dx in range(3):
        for dy in range(3):
            taps[(2 - dy) * CH : (2 - dy) * CH + OUTC, :] = d_out[dy * 3 + dx].astype(F32)
        base = taps[...].T
        for e in range(7, 17):
            moved = pltpu.roll(base, ((e - 9) * CH) % 128, axis=1)
            if e < 9:
                moved = jnp.where(lane128 < (e - 6) * CH, moved, 0.0)
            if e > 14:
                moved = jnp.where(lane128 >= (e - 9) * CH, moved, 0.0)
            wb_vel[(e - 7) * DIF : (e - 6) * DIF, dx * 128 : (dx + 1) * 128] = moved.astype(BF16)

    lane_row = lane256 // CH
    lane_ok = jnp.zeros((1, 256), F32)
    seed = jnp.zeros((1, 256), jnp.int32)
    for r in range(16):
        row = lat * ROWS - 4 + r
        here = seeds[jnp.clip(row, 0, BAND_ROWS - 1)]
        seed = jnp.where(lane_row == r, here, seed)
        lane_ok = jnp.where(lane_row == r, row_ok(4 + r), lane_ok)

    def shift(values, dx):
        count = values.shape[0]
        spot = lax.broadcasted_iota(jnp.int32, values.shape, 0)
        if dx == 0:
            return jnp.where(spot == 0, 0.0, pltpu.roll(values, 1, axis=0))
        if dx == 2:
            return jnp.where(spot == count - 1, 0.0, pltpu.roll(values, count - 1, axis=0))
        return values

    def put_part(part, values):
        for dx in range(3):
            moved = shift(values, dx)
            at = part * 384 + dx * 128
            parts[0, :, at : at + 128] = moved[:, :128].astype(BF16)
            parts[1, :, at : at + 128] = pltpu.roll(moved, 192, axis=1)[:, :128].astype(BF16)
            parts[2, :, at : at + 128] = moved[:, 128:].astype(BF16)

    def noise_rows(i, carry):
        at = pl.multiple_of(i * 32, 32)
        column = lon * COLS - MARGIN + at + lax.broadcasted_iota(jnp.int32, (32, 256), 0)
        column = jnp.where(column < 0, column + BAND_COLS, column)
        column = jnp.where(column >= BAND_COLS, column - BAND_COLS, column)
        channel = lax.broadcasted_iota(jnp.int32, (32, 256), 1) % CH
        start = seed ^ ((column * OUTC + channel) * 1640531527)
        total = jnp.zeros((32, 256), jnp.int32)
        for turn in range(4):
            total = total + (hashed(start + turn * 374761393) & 65535)
        uniform = total.astype(F32) * (1.0 / 65536.0) + 4.0 / 131072.0
        noise_keep[pl.ds(at, 32), :] = (uniform - 2.0) * 1.7320508075688772 * lane_ok
        return carry

    lax.fori_loop(0, PATCH // 32, noise_rows, 0)
    put_part(0, noise_keep[...])

    pl.semaphore_wait(barrier, ALL - 1)

    def around(k):
        dlon, dlat = AROUND[k]
        target = {"lon": lax.rem(lon + dlon + LON, LON), "lat": lax.rem(lat + dlat + LAT, LAT)}
        if dlon == 0:
            src, dst = own16, tall.at[k]
        elif dlon == 1:
            src, dst = own16.at[:, 128:256], wide.at[k - 2]
        else:
            src, dst = own16.at[:, 0:128], wide.at[k - 2]
        return pltpu.make_async_remote_copy(
            src_ref=src,
            dst_ref=dst,
            send_sem=in_send.at[k],
            recv_sem=in_recv.at[k],
            device_id=target,
            device_id_type=MESH,
        )

    order = (2, 4, 5, 7, 3, 6, 0, 1)
    copies = {k: around(k) for k in order}
    for k in order:
        copies[k].start()
    for k in order:
        copies[k].wait_recv()

    def assemble(centre, left, right):
        lane = lax.broadcasted_iota(jnp.int32, (128, 384), 1)
        zeros = jnp.zeros((128, 128), F32)
        mid = pltpu.roll(jnp.concatenate([centre, zeros], axis=1), SIDE, axis=1)
        low = pltpu.roll(jnp.concatenate([left, zeros, zeros], axis=1), 384 - 24, axis=1)
        high = pltpu.roll(jnp.concatenate([right, zeros, zeros], axis=1), SIDE + COLS, axis=1)
        inner = jnp.where(lane < SIDE + COLS, mid, jnp.where(lane < W, high, 0.0))
        return jnp.where(lane < SIDE, low, inner)

    up = assemble(tall[1].astype(F32), wide[7 - 2].astype(F32), wide[4 - 2].astype(F32))
    mid = assemble(own16[...].astype(F32), wide[6 - 2].astype(F32), wide[3 - 2].astype(F32))
    down = assemble(tall[0].astype(F32), wide[5 - 2].astype(F32), wide[2 - 2].astype(F32))
    up = jnp.where(lat == 0, 0.0, up)
    down = jnp.where(lat == LAT - 1, 0.0, down)
    xt = jnp.concatenate([up.T, mid.T, down.T], axis=1)[:W]
    xt_far = pltpu.roll(xt, 320, axis=1)
    for dx in range(3):
        if dx == 0:
            near, far = pltpu.roll(xt, 1, axis=0), pltpu.roll(xt_far, 1, axis=0)
        elif dx == 2:
            near, far = pltpu.roll(xt, W - 1, axis=0), pltpu.roll(xt_far, W - 1, axis=0)
        else:
            near, far = xt, xt_far
        for win in range(5):
            source = (near, far)[win % 2]
            at = (win // 2) * 128
            xw[win, :, dx * 128 : (dx + 1) * 128] = source[:, at : at + 128].astype(BF16)

    def first_rows(win, low, high):
        out = jnp.dot(
            xw[win], wb_in[:, low * REG : high * REG], preferred_element_type=F32
        ).astype(BF16)
        s = jnp.zeros((8, REG), F32)
        q = jnp.zeros((8, REG), F32)
        for p in range(low, high):
            e = win * 4 + 1 + p
            row = out[:, (p - low) * REG : (p - low + 1) * REG]
            first[e * W : (e + 1) * W, :] = row
            if 8 <= e < 16:
                cell = row[SIDE : SIDE + COLS].astype(F32)
                s = s + fold(cell)
                q = q + fold(cell * cell)
        return s, q

    def send_band(which, s, q, recv):
        stat_send[which, 0:1, :] = jnp.sum(s, axis=0, keepdims=True)
        stat_send[which, 1:2, :] = jnp.sum(q, axis=0, keepdims=True)

        def one(target, slot):
            pltpu.make_async_remote_copy(
                src_ref=stat_send.at[which, pl.ds(0, 2)],
                dst_ref=recv.at[slot],
                send_sem=st_send.at[which],
                recv_sem=st_recv.at[which],
                device_id=target,
                device_id_type=MESH,
            ).start()

        to_all(one)

    def band_scale(which, recv):
        pltpu.make_async_copy(recv, recv, st_recv.at[which]).wait()
        stat_send[4 + which, 0:2, :] = stat_send[which, 0:2, :] + jnp.sum(recv[...], axis=0)
        total = all_groups(stat_send[4 + which], REG // 32)
        return scale_shift(
            total[0:1], total[1:2], float(BAND_ROWS * BAND_COLS * (REG // 32))
        )

    def send_patch(which, s, q, recv):
        s = jnp.sum(s, axis=0, keepdims=True)
        q = jnp.sum(q, axis=0, keepdims=True)
        stat_send[which, 0:1, :] = s[:, :128]
        stat_send[which, 1:2, :] = s[:, 128:]
        stat_send[which, 2:3, :] = q[:, :128]
        stat_send[which, 3:4, :] = q[:, 128:]
        for step in range(1, LAT):
            pltpu.make_async_remote_copy(
                src_ref=stat_send.at[which, pl.ds(0, 4)],
                dst_ref=recv.at[step - 1],
                send_sem=st_send.at[which],
                recv_sem=st_recv.at[which],
                device_id={"lat": lax.rem(lat + step, LAT)},
                device_id_type=MESH,
            ).start()

    def patch_scale(which, recv):
        pltpu.make_async_copy(recv, recv, st_recv.at[which]).wait()
        stat_send[4 + which, 0:4, :] = stat_send[which, 0:4, :] + jnp.sum(recv[...], axis=0)
        total = all_groups(stat_send[4 + which], DIF // 32)
        sums = jnp.concatenate([total[0:1], total[1:2]], axis=1)
        squares = jnp.concatenate([total[2:3], total[3:4]], axis=1)
        return scale_shift(sums, squares, float(BAND_ROWS * PATCH * (DIF // 32)))

    stats = [first_rows(1, 3, 6), first_rows(2, 2, 4), first_rows(3, 0, 3)]
    stat_send[...] = jnp.zeros_like(stat_send)
    send_band(0, sum(s for s, _ in stats), sum(q for _, q in stats), stat_one)

    first_rows(0, 0, 6)
    first_rows(1, 2, 3)
    first_rows(3, 3, 6)
    first_rows(4, 2, 6)
    own_xt = xt_far[OFF : OFF + PATCH, :256]
    put_part(1, own_xt)

    def patch_rows(win):
        return ((3, 6), (2, 4), (0, 3))[win]

    def rest_rows(win):
        return ((0, 3), None, (3, 6))[win]

    for win in range(3):
        for span in (patch_rows(win), rest_rows(win)):
            if span is None:
                continue
            low, high = span
            out = jnp.dot(
                parts[win, :, 0:768],
                wb_patch[0:768, low * DIF : high * DIF],
                preferred_element_type=F32,
            )
            for p in range(low, high):
                e = win * 4 + 5 + p
                partial[(e - 5) * PATCH : (e - 4) * PATCH, :] = out[
                    :, (p - low) * DIF : (p - low + 1) * DIF
                ]

    def activate_band(source, a, b, e):
        ok = row_ok(e)
        at = at_row(e, W)
        half = source[pl.ds(at, W), :].astype(F32) * (a * ok) + b * ok
        out = half_silu(half)
        act[0, pl.ds(at, W), :] = pltpu.roll(out, 1, axis=0).astype(BF16)
        act[1, pl.ds(at, W), :] = out.astype(BF16)
        act[2, pl.ds(at, W), :] = pltpu.roll(out, W - 1, axis=0).astype(BF16)

    def loop(count, body):
        lax.fori_loop(0, count, lambda i, c: (body(i), c)[1], 0)

    def conv_band(weight, e, pairs):
        def rows_of(q, dx):
            return [
                act[dx, pl.ds(at_row(e + 2 * k + q - 1, W), W), :] for k in range(pairs)
            ]

        lhs = jnp.concatenate(
            [
                jnp.concatenate(rows_of(q, dx), axis=0)
                for q in range(4)
                for dx in range(3)
            ],
            axis=1,
        )
        out = jnp.dot(lhs, weight[...], preferred_element_type=F32)
        return [
            out[(r // 2) * W : (r // 2 + 1) * W, (r % 2) * REG : (r % 2 + 1) * REG]
            for r in range(2 * pairs)
        ]

    a, b = band_scale(0, stat_one)
    loop(10, lambda i: activate_band(first, a, b, i + 7))
    for load in loads[0]:
        load.wait()

    s = jnp.zeros((8, REG), F32)
    q = jnp.zeros((8, REG), F32)
    for i, out in enumerate(conv_band(w_one, 8, 4)):
        out = out.astype(BF16)
        second[(8 + i) * W : (9 + i) * W, :] = out
        cell = out[SIDE : SIDE + COLS].astype(F32)
        s = s + fold(cell)
        q = q + fold(cell * cell)
    send_band(1, s, q, stat_two)

    def second_rest(i):
        e = 2 + i * 14
        for k, out in enumerate(conv_band(w_one, e, 3)):
            second[pl.ds(at_row(e + k, W), W), :] = out.astype(BF16)

    loop(12, lambda i: activate_band(first, a, b, 1 + i + (i // 6) * 10))
    loop(2, second_rest)

    a2, b2 = band_scale(1, stat_two)
    loop(14, lambda i: activate_band(second, a2, b2, i + 5))
    for load in loads[1]:
        load.wait()

    def third_rows(e, pairs):
        for k, out in enumerate(conv_band(w_two, e, pairs)):
            at = at_row(e + k, W)
            out = first[pl.ds(at, W), :].astype(F32) + out
            third[pl.ds(at, W), :] = (out * row_ok(e + k)).astype(BF16)

    loop(2, lambda i: third_rows(6 + 6 * i, 3))

    def mean_terms(low, high):
        lhs = jnp.concatenate([third[e * W : (e + 1) * W, :] for e in range(low, high)], axis=1)
        return [
            jnp.dot(
                lhs,
                wb_mean[(low - 3) * REG : (high - 3) * REG, dx * 256 : (dx + 1) * 256],
                preferred_element_type=F32,
            )
            for dx in range(3)
        ]

    def put_mean():
        total = (
            pltpu.roll(mean_acc[0], 1, axis=0)
            + mean_acc[1]
            + pltpu.roll(mean_acc[2], W - 1, axis=0)
        )[OFF : OFF + PATCH]
        put_part(2, total * lane_ok)
        return total

    def patch_first_rows(win, span):
        low, high = span
        out = jnp.dot(
            parts[win, :, 768:1152],
            wb_patch[768:1152, low * DIF : high * DIF],
            preferred_element_type=F32,
        )
        s = jnp.zeros((8, DIF), F32)
        q = jnp.zeros((8, DIF), F32)
        for p in range(low, high):
            e = win * 4 + 5 + p
            at = (e - 5) * PATCH
            row = out[:, (p - low) * DIF : (p - low + 1) * DIF] + partial[at : at + PATCH, :]
            row = row.astype(BF16)
            p_first[at : at + PATCH, :] = row
            if 8 <= e < 16:
                cell = row.astype(F32)
                s = s + fold(cell)
                q = q + fold(cell * cell)
        return s, q

    for dx, term in enumerate(mean_terms(6, 18)):
        mean_acc[dx] = term
    put_mean()
    stats = [patch_first_rows(win, patch_rows(win)) for win in range(3)]
    send_patch(2, sum(s for s, _ in stats), sum(q for _, q in stats), stat_three)

    def activate_rest(i):
        activate_band(second, a2, b2, 2 + i + (i // 3) * 14)

    loop(6, activate_rest)
    loop(2, lambda i: third_rows(3 + 14 * i, 2))
    for low, high in ((3, 6), (18, 21)):
        for dx, term in enumerate(mean_terms(low, high)):
            mean_acc[dx] = mean_acc[dx] + term
    mean_all = put_mean()
    mean_own = pltpu.roll(mean_all, 192, axis=1)[:, :128]
    noise_own = pltpu.roll(noise_keep[...], 192, axis=1)[:, :128]
    base = mean_own + noise_own

    def put_out(out_ref, values):
        flat = pltpu.roll(values.T, PATCH - MARGIN, axis=1)[:, :COLS]
        for r in range(ROWS):
            out_ref[:, r, :] = flat[r * CH : r * CH + OUTC, :]

    put_out(mean_out, mean_own)
    pad32[...] = base
    patch_first_rows(0, rest_rows(0))
    patch_first_rows(2, rest_rows(2))

    def activate_patch(source, shift_row, a, b, e):
        ok = row_ok(e)
        half = source[pl.ds(at_row(e - shift_row, PATCH), PATCH), :].astype(F32) * (a * ok) + b * ok
        out = half_silu(half)
        at = at_row(e - 5, PATCH)
        for dx in range(3):
            p_act[dx, pl.ds(at, PATCH), :] = shift(out, dx).astype(BF16)

    def conv_patch(weight, e, rows):
        lhs = jnp.concatenate(
            [
                p_act[dx, pl.ds(at_row(e + dy - 6, PATCH), rows * PATCH), :]
                for dy in range(3)
                for dx in range(3)
            ],
            axis=1,
        )
        return jnp.dot(lhs, weight[...], preferred_element_type=F32)

    a3, b3 = patch_scale(2, stat_three)
    loop(10, lambda i: activate_patch(p_first, 5, a3, b3, i + 7))
    for load in loads[2]:
        load.wait()

    def p_second_own(i, carry):
        s, q = carry
        e = 8 + 4 * i
        out = conv_patch(d_one, e, 4).astype(BF16)
        p_second[pl.ds(at_row(e - 6, PATCH), 4 * PATCH), :] = out
        cell = out.astype(F32)
        return s + fold(cell), q + fold(cell * cell)

    zero = jnp.zeros((8, DIF), F32)
    s, q = lax.fori_loop(0, 2, p_second_own, (zero, zero))
    send_patch(3, s, q, stat_four)

    def p_second_rest(i):
        e = 6 + i * 10
        out = conv_patch(d_one, e, 2).astype(BF16)
        p_second[pl.ds(at_row(e - 6, PATCH), 2 * PATCH), :] = out

    loop(4, lambda i: activate_patch(p_first, 5, a3, b3, 5 + i + (i // 2) * 10))
    loop(2, p_second_rest)

    a4, b4 = patch_scale(3, stat_four)
    loop(12, lambda i: activate_patch(p_second, 6, a4, b4, i + 6))
    for load in loads[3]:
        load.wait()

    def p_third_rows(i):
        e = 7 + 5 * i
        conv = conv_patch(d_two, e, 5)
        for k in range(5):
            out = p_first[pl.ds(at_row(e + k - 5, PATCH), PATCH), :].astype(F32)
            out = (out + conv[k * PATCH : (k + 1) * PATCH]) * row_ok(e + k)
            p_third[pl.ds(at_row(e + k - 7, PATCH), PATCH), :] = out.astype(BF16)

    loop(2, p_third_rows)

    lhs = jnp.concatenate([p_third[e * PATCH : (e + 1) * PATCH, :] for e in range(10)], axis=1)
    out = jnp.dot(lhs, wb_vel[...], preferred_element_type=F32)
    velocity = shift(out[:, 0:128], 0) + out[:, 128:256] + shift(out[:, 256:384], 2)
    edge_send[0] = velocity[0:MARGIN]
    edge_send[1] = velocity[PATCH - MARGIN : PATCH]
    edges = [
        pltpu.make_async_remote_copy(
            src_ref=edge_send.at[k],
            dst_ref=edge_recv.at[k],
            send_sem=e_send.at[k],
            recv_sem=e_recv.at[k],
            device_id={"lon": lax.rem(lon + LON + step, LON)},
            device_id_type=MESH,
        )
        for k, step in ((0, -1), (1, 1))
    ]
    for edge in edges:
        edge.start()
    for k in order:
        copies[k].wait_send()
    for which, recv in enumerate((stat_one, stat_two, stat_three, stat_four)):
        pltpu.make_async_copy(recv, recv, st_send.at[which]).wait()
    for edge in edges:
        edge.wait()
    from_left = velocity[MARGIN : 2 * MARGIN] + edge_recv[1]
    from_right = velocity[COLS : COLS + MARGIN] + edge_recv[0]
    total = jnp.concatenate(
        [
            velocity[0:MARGIN],
            from_left * 0.5,
            velocity[2 * MARGIN : COLS],
            from_right * 0.5,
            velocity[COLS + MARGIN :],
        ],
        axis=0,
    )
    put_out(field_out, pad32[...] + total)


def hand_over(mean_in, field_in, mean_out, field_out):
    mean_out[...] = mean_in[...]
    field_out[...] = field_in[...]


def on_device(coarse, static, noise_seeds, w_in, w_one, w_two, w_out, d_in, d_one, d_two, d_out):
    vmem = pl.BlockSpec(memory_space=pltpu.VMEM)
    smem = pl.BlockSpec(memory_space=pltpu.SMEM)
    hbm = pl.BlockSpec(memory_space=pl.ANY)
    out = jax.ShapeDtypeStruct((OUTC, ROWS, COLS), F32)
    results = pl.pallas_call(
        kernel,
        out_shape=(out, out),
        in_specs=[hbm, hbm, smem, vmem, hbm, hbm, vmem, vmem, hbm, hbm, vmem],
        out_specs=(vmem, vmem),
        scratch_shapes=[
            pltpu.VMEM((OUTC, ROWS, COLS), F32),
            pltpu.VMEM((CH - OUTC, ROWS, COLS), F32),
            pltpu.VMEM((12 * REG, 2 * REG), BF16),
            pltpu.VMEM((12 * REG, 2 * REG), BF16),
            pltpu.VMEM((9 * DIF, DIF), BF16),
            pltpu.VMEM((9 * DIF, DIF), BF16),
            pltpu.VMEM((128, 256), F32),
            pltpu.VMEM((128, 256), BF16),
            pltpu.VMEM((2, 128, 256), BF16),
            pltpu.VMEM((6, 128, 128), BF16),
            pltpu.VMEM((5, W, 384), BF16),
            pltpu.VMEM((384, 6 * REG), BF16),
            pltpu.VMEM((1152, 6 * DIF), BF16),
            pltpu.VMEM((18 * REG, 768), BF16),
            pltpu.VMEM((10 * DIF, 384), BF16),
            pltpu.VMEM((FRAME * W, REG), BF16),
            pltpu.VMEM((FRAME * W, REG), BF16),
            pltpu.VMEM((FRAME * W, REG), BF16),
            pltpu.VMEM((3, FRAME * W, REG), BF16),
            pltpu.VMEM((PATCH, 256), F32),
            pltpu.VMEM((3, PATCH, 1152), BF16),
            pltpu.VMEM((14 * PATCH, DIF), F32),
            pltpu.VMEM((3, W, 256), F32),
            pltpu.VMEM((14 * PATCH, DIF), BF16),
            pltpu.VMEM((12 * PATCH, DIF), BF16),
            pltpu.VMEM((10 * PATCH, DIF), BF16),
            pltpu.VMEM((3, 14 * PATCH, DIF), BF16),
            pltpu.VMEM((256, 128), F32),
            pltpu.VMEM((128, DIF), F32),
            pltpu.VMEM((2, MARGIN, 128), F32),
            pltpu.VMEM((2, MARGIN, 128), F32),
            pltpu.VMEM((8, 8, 128), F32),
            pltpu.VMEM((ALL - 1, 2, 128), F32),
            pltpu.VMEM((ALL - 1, 2, 128), F32),
            pltpu.VMEM((LAT - 1, 4, 128), F32),
            pltpu.VMEM((LAT - 1, 4, 128), F32),
            pltpu.SemaphoreType.DMA((8,)),
            pltpu.SemaphoreType.DMA((8,)),
            pltpu.SemaphoreType.DMA((8,)),
            pltpu.SemaphoreType.DMA((4,)),
            pltpu.SemaphoreType.DMA((4,)),
            pltpu.SemaphoreType.DMA((2,)),
            pltpu.SemaphoreType.DMA((2,)),
        ],
        compiler_params=pltpu.CompilerParams(
            collective_id=0, has_side_effects=True, vmem_limit_bytes=60 * 1024 * 1024
        ),
    )(
        coarse,
        static,
        noise_seeds,
        w_in.reshape(9, CH, REG),
        w_one.reshape(9 * REG, REG),
        w_two.reshape(9 * REG, REG),
        jnp.transpose(w_out.reshape(9, REG, OUTC), (0, 2, 1)),
        d_in.reshape(9, 40, DIF),
        d_one.reshape(9 * DIF, DIF),
        d_two.reshape(9 * DIF, DIF),
        jnp.transpose(d_out.reshape(9, DIF, OUTC), (0, 2, 1)),
    )
    return pl.pallas_call(
        hand_over,
        out_shape=(out, out),
        in_specs=[vmem, vmem],
        out_specs=(vmem, vmem),
    )(*results)


def solution(mesh):
    brick = P(None, "lat", "lon")
    return jax.shard_map(
        on_device,
        mesh=mesh,
        in_specs=(brick, brick) + (P(),) * 9,
        out_specs=(brick, brick),
        check_vma=False,
    )
```

```python
import functools

import jax
import jax.numpy as jnp
from jax import lax
from jax.experimental import pallas as pl
from jax.experimental.pallas import tpu as pltpu
from jax.sharding import PartitionSpec as P

MESH = pl.DeviceIdType.MESH
F32 = jnp.float32
BF16 = jnp.bfloat16

LON, LAT = 16, 8
ALL = LON * LAT
ROWS = 8
COLS = 192
BAND_ROWS = ROWS * LAT
BAND_COLS = COLS * LON
MARGIN = 32
PATCH = COLS + 2 * MARGIN
SIDE = 40
W = COLS + 2 * SIDE
OFF = SIDE - MARGIN
FRAME = 3 * ROWS
CH = 16
REG = 128
DIF = 256
OUTC = 12
STEPS = (2, 1, 3, 0)
P_SECOND_GROUPS = ((8, 4), (12, 4))
P_THIRD_GROUPS = ((7, 4), (11, 4), (15, 2))
SECOND_GROUPS = ((8, 2), (12, 2))
THIRD_GROUPS = ((6, 2), (10, 2), (14, 2))
EPS = 1e-05

AROUND = ((0, -1), (0, 1), (-1, -1), (-1, 0), (-1, 1), (1, -1), (1, 0), (1, 1))


def hashed(value):
    for _ in range(2):
        value = value ^ (lax.shift_right_logical(value, 16))
        value = value * 73244475
    return value ^ (lax.shift_right_logical(value, 16))


def at_row(row, width):
    return row * width if isinstance(row, int) else pl.multiple_of(row * width, 16)


def all_groups(stats, size):
    lane = lax.broadcasted_iota(jnp.int32, stats.shape, 1)
    step = 1
    while step < size:
        up = pltpu.roll(stats, 128 - step, axis=1)
        down = pltpu.roll(stats, step, axis=1)
        stats = stats + jnp.where((lane // step) % 2 == 0, up, down)
        step *= 2
    return stats


def scale_shift(sums, squares, count):
    mean = sums / count
    scale = lax.rsqrt(squares / count - mean * mean + EPS)
    return 0.5 * scale, -0.5 * scale * mean


def half_silu(half):
    return half + half * jnp.tanh(half)


def fold(values):
    return jnp.sum(values.reshape(values.shape[0] // 8, 8, values.shape[1]), axis=0)


def kernel(
    coarse_hbm,
    static_hbm,
    seeds,
    w_in_hbm,
    w_one_hbm,
    w_two_hbm,
    w_out_hbm,
    d_in_hbm,
    d_one_hbm,
    d_two_hbm,
    d_out_hbm,
    mean_out,
    field_out,
    coarse,
    static,
    w_in,
    w_out,
    d_in,
    d_out,
    w_one,
    w_two,
    d_one,
    d_two,
    own32,
    own16,
    tall,
    wide,
    xw,
    wb_in,
    wb_patch,
    wb_mean,
    wb_vel,
    first,
    second,
    third,
    act,
    noise_keep,
    parts,
    partial,
    mean_acc,
    p_first,
    p_second,
    p_third,
    p_act,
    pad32,
    taps,
    edge_send,
    edge_recv,
    stat_send,
    stat_one,
    stat_two,
    stat_three,
    stat_four,
    w_sem,
    in_send,
    in_recv,
    st_send,
    st_recv,
    e_send,
    e_recv,
):
    lon = lax.axis_index("lon")
    lat = lax.axis_index("lat")

    core = lax.rem(lon, 2)
    y = lax.rem(lon // 2, 4)
    x = lax.rem(lat, 4)
    z = (lon // 8) * 2 + lat // 4

    def chip(dz, dy, dx):
        there = lax.rem(z + dz, 4)
        far_lon = (there // 2) * 8 + lax.rem(y + dy, 4) * 2
        return far_lon, lax.rem(there, 2) * 4 + lax.rem(x + dx, 4)

    def reach(i):
        return jnp.where(i == 0, 2, jnp.where(i == 3, 0, jnp.where(i == 1, 1, 3)))

    def to_all(action):
        def some(i, carry):
            dz, dy = reach(i // 4), reach(lax.rem(i, 4))
            for j, dx in enumerate(STEPS):
                far_lon, far_lat = chip(dz, dy, dx)
                for k in range(2):
                    target = {"lon": far_lon + (1 - core if k == 0 else core), "lat": far_lat}
                    action(target, i * 8 + j * 2 + k)
            return carry

        lax.fori_loop(0, 15, some, 0)
        for j, dx in enumerate(STEPS):
            far_lon, far_lat = chip(0, 0, dx)
            for k in range(2):
                if (j, k) != (3, 1):
                    target = {"lon": far_lon + (1 - core if k == 0 else core), "lat": far_lat}
                    action(target, 120 + j * 2 + k)

    def row_ok(e):
        row = lat * ROWS - ROWS + e
        return jnp.where((row >= 0) & (row < BAND_ROWS), 1.0, 0.0).astype(F32)

    barrier = pltpu.get_barrier_semaphore()

    to_all(
        lambda target, slot: pl.semaphore_signal(
            barrier, inc=1, device_id=target, device_id_type=MESH
        )
    )

    wide_w = ((w_one_hbm, w_one), (w_two_hbm, w_two))
    loads = []
    for i, (src, dst) in enumerate(wide_w):
        dst[3 * 384 : 4 * 384, 0:128] = jnp.zeros((384, 128), BF16)
        dst[0:384, 128:256] = jnp.zeros((384, 128), BF16)
        loads.append(
            [
                pltpu.make_async_copy(
                    src,
                    dst.at[p * 384 : p * 384 + 9 * REG, p * 128 : (p + 1) * 128],
                    w_sem.at[i * 2 + p],
                )
                for p in range(2)
            ]
        )
    loads.append([pltpu.make_async_copy(d_one_hbm, d_one, w_sem.at[4])])
    loads.append([pltpu.make_async_copy(d_two_hbm, d_two, w_sem.at[5])])
    near = [
        pltpu.make_async_copy(coarse_hbm, coarse, w_sem.at[6]),
        pltpu.make_async_copy(static_hbm, static, w_sem.at[7]),
        pltpu.make_async_copy(w_in_hbm, w_in, w_sem.at[8]),
        pltpu.make_async_copy(w_out_hbm, w_out, w_sem.at[9]),
        pltpu.make_async_copy(d_in_hbm, d_in, w_sem.at[10]),
        pltpu.make_async_copy(d_out_hbm, d_out, w_sem.at[11]),
    ]
    for load in near:
        load.start()
    for group in loads:
        for load in group:
            load.start()
    for load in near:
        load.wait()
    own32[...] = jnp.zeros_like(own32)
    for r in range(ROWS):
        own32[r * CH : r * CH + 12, 0:COLS] = coarse[:, r, :]
        own32[r * CH + 12 : r * CH + 16, 0:COLS] = static[:, r, :]
    own16[...] = own32[...].astype(BF16)

    wb_in[...] = jnp.zeros_like(wb_in)
    for p in range(6):
        for dy in range(3):
            for dx in range(3):
                at = dx * 128 + (p + dy) * CH
                wb_in[at : at + CH, p * REG : (p + 1) * REG] = w_in[dy * 3 + dx]
    wb_patch[...] = jnp.zeros_like(wb_patch)
    low_rows = lax.broadcasted_iota(jnp.int32, (40, DIF), 0) < OUTC
    for dy in range(3):
        for dx in range(3):
            raw = d_in[dy * 3 + dx].astype(F32)
            pieces = (
                jnp.where(low_rows, raw, 0.0)[:CH].astype(BF16),
                raw[24:40].astype(BF16),
                jnp.where(low_rows, pltpu.roll(raw, 28, axis=0), 0.0)[:CH].astype(BF16),
            )
            for part, piece in enumerate(pieces):
                for p in range(6):
                    at = part * 384 + dx * 128 + (p + dy) * CH
                    wb_patch[at : at + CH, p * DIF : (p + 1) * DIF] = piece
    taps[...] = jnp.zeros_like(taps)
    lane256 = lax.broadcasted_iota(jnp.int32, (1, 256), 1)
    lane128 = lax.broadcasted_iota(jnp.int32, (1, 128), 1)
    for dx in range(3):
        for dy in range(3):
            taps[(2 - dy) * CH : (2 - dy) * CH + OUTC, 0:REG] = w_out[dy * 3 + dx].astype(F32)
        base = jnp.concatenate([taps[:, 0:REG].T, jnp.zeros((REG, 128), F32)], axis=1)
        for e in range(3, 21):
            moved = pltpu.roll(base, ((e - 5) * CH) % 256, axis=1)
            if e < 5:
                moved = jnp.where(lane256 < (e - 2) * CH, moved, 0.0)
            if e > 18:
                moved = jnp.where(lane256 >= (e - 5) * CH, moved, 0.0)
            wb_mean[(e - 3) * REG : (e - 2) * REG, dx * 256 : (dx + 1) * 256] = moved.astype(BF16)
    for dx in range(3):
        for dy in range(3):
            taps[(2 - dy) * CH : (2 - dy) * CH + OUTC, :] = d_out[dy * 3 + dx].astype(F32)
        base = taps[...].T
        for e in range(7, 17):
            moved = pltpu.roll(base, ((e - 9) * CH) % 128, axis=1)
            if e < 9:
                moved = jnp.where(lane128 < (e - 6) * CH, moved, 0.0)
            if e > 14:
                moved = jnp.where(lane128 >= (e - 9) * CH, moved, 0.0)
            wb_vel[(e - 7) * DIF : (e - 6) * DIF, dx * 128 : (dx + 1) * 128] = moved.astype(BF16)

    lane_row = lane256 // CH
    lane_ok = jnp.zeros((1, 256), F32)
    seed = jnp.zeros((1, 256), jnp.int32)
    for r in range(16):
        row = lat * ROWS - 4 + r
        here = seeds[jnp.clip(row, 0, BAND_ROWS - 1)]
        seed = jnp.where(lane_row == r, here, seed)
        lane_ok = jnp.where(lane_row == r, row_ok(4 + r), lane_ok)

    def shift(values, dx):
        count = values.shape[0]
        spot = lax.broadcasted_iota(jnp.int32, values.shape, 0)
        if dx == 0:
            return jnp.where(spot == 0, 0.0, pltpu.roll(values, 1, axis=0))
        if dx == 2:
            return jnp.where(spot == count - 1, 0.0, pltpu.roll(values, count - 1, axis=0))
        return values

    spot_low = lax.broadcasted_iota(jnp.int32, (16, 128), 0)

    def put_part(part, values):
        windows = (values[:, :128], pltpu.roll(values, 192, axis=1)[:, :128], values[:, 128:])
        for win, block in enumerate(windows):
            at = part * 384
            later = pltpu.roll(block, 1, axis=0)
            sooner = pltpu.roll(block, PATCH - 1, axis=0)
            parts[win, 0:16, at : at + 128] = jnp.where(spot_low == 0, 0.0, later[:16]).astype(BF16)
            parts[win, 16:, at : at + 128] = later[16:].astype(BF16)
            parts[win, :, at + 128 : at + 256] = block.astype(BF16)
            parts[win, :-16, at + 256 : at + 384] = sooner[:-16].astype(BF16)
            parts[win, PATCH - 16 :, at + 256 : at + 384] = jnp.where(
                spot_low == 15, 0.0, sooner[-16:]
            ).astype(BF16)

    def noise_rows(i, carry):
        at = pl.multiple_of(i * 32, 32)
        column = lon * COLS - MARGIN + at + lax.broadcasted_iota(jnp.int32, (32, 256), 0)
        column = jnp.where(column < 0, column + BAND_COLS, column)
        column = jnp.where(column >= BAND_COLS, column - BAND_COLS, column)
        channel = lax.broadcasted_iota(jnp.int32, (32, 256), 1) % CH
        start = seed ^ ((column * OUTC + channel) * 1640531527)
        total = jnp.zeros((32, 256), jnp.int32)
        for turn in range(4):
            total = total + (hashed(start + turn * 374761393) & 65535)
        uniform = total.astype(F32) * (1.0 / 65536.0) + 4.0 / 131072.0
        noise_keep[pl.ds(at, 32), :] = (uniform - 2.0) * 1.7320508075688772 * lane_ok
        return carry

    lax.fori_loop(0, PATCH // 32, noise_rows, 0)
    put_part(0, noise_keep[...])

    pl.semaphore_wait(barrier, ALL - 1)

    def around(k):
        dlon, dlat = AROUND[k]
        target = {"lon": lax.rem(lon + dlon + LON, LON), "lat": lax.rem(lat + dlat + LAT, LAT)}
        if dlon == 0:
            src, dst = own16, tall.at[k]
        elif dlon == 1:
            src, dst = own16.at[:, 128:256], wide.at[k - 2]
        else:
            src, dst = own16.at[:, 0:128], wide.at[k - 2]
        return pltpu.make_async_remote_copy(
            src_ref=src,
            dst_ref=dst,
            send_sem=in_send.at[k],
            recv_sem=in_recv.at[k],
            device_id=target,
            device_id_type=MESH,
        )

    order = (2, 4, 5, 7, 3, 6, 0, 1)
    copies = {k: around(k) for k in order}
    for k in order:
        copies[k].start()
    for k in order:
        copies[k].wait_recv()

    def assemble(centre, left, right):
        lane = lax.broadcasted_iota(jnp.int32, (128, 128), 1)
        low = pltpu.roll(left, 128 - 24, axis=1)
        one = pltpu.roll(centre[:, :128], SIDE, axis=1)
        two = pltpu.roll(centre[:, 128:], SIDE, axis=1)
        high = pltpu.roll(right, SIDE + COLS - 128, axis=1)
        return jnp.concatenate(
            [
                jnp.where(lane < SIDE, low, one),
                jnp.where(lane < SIDE, one, jnp.where(lane < SIDE + COLS - 128, two, high)),
                jnp.where(lane < W - 256, high, 0.0),
            ],
            axis=1,
        )

    up = assemble(tall[1].astype(F32), wide[7 - 2].astype(F32), wide[4 - 2].astype(F32))
    mid = assemble(own16[...].astype(F32), wide[6 - 2].astype(F32), wide[3 - 2].astype(F32))
    down = assemble(tall[0].astype(F32), wide[5 - 2].astype(F32), wide[2 - 2].astype(F32))
    up = jnp.where(lat == 0, 0.0, up)
    down = jnp.where(lat == LAT - 1, 0.0, down)
    xt = jnp.concatenate([up.T, mid.T, down.T], axis=1)[:W]
    xt_far = pltpu.roll(xt, 320, axis=1)

    def put_window(win):
        at = (win // 2) * 128
        block = (xt, xt_far)[win % 2][:, at : at + 128]
        xw[win, :, 0:128] = pltpu.roll(block, 1, axis=0).astype(BF16)
        xw[win, :, 128:256] = block.astype(BF16)
        xw[win, :, 256:384] = pltpu.roll(block, W - 1, axis=0).astype(BF16)

    for win in (1, 2, 3):
        put_window(win)

    def first_rows(win, low, high):
        out = jnp.dot(
            xw[win], wb_in[:, low * REG : high * REG], preferred_element_type=F32
        ).astype(BF16)
        s = jnp.zeros((8, REG), F32)
        q = jnp.zeros((8, REG), F32)
        for p in range(low, high):
            e = win * 4 + 1 + p
            row = out[:, (p - low) * REG : (p - low + 1) * REG]
            first[e * W : (e + 1) * W, :] = row
            if 8 <= e < 16:
                cell = row[SIDE : SIDE + COLS].astype(F32)
                s = s + fold(cell)
                q = q + fold(cell * cell)
        return s, q

    def send_band(which, s, q, recv):
        stat_send[which, 0:1, :] = jnp.sum(s, axis=0, keepdims=True)
        stat_send[which, 1:2, :] = jnp.sum(q, axis=0, keepdims=True)

        def one(target, slot):
            pltpu.make_async_remote_copy(
                src_ref=stat_send.at[which, pl.ds(0, 2)],
                dst_ref=recv.at[slot],
                send_sem=st_send.at[which],
                recv_sem=st_recv.at[which],
                device_id=target,
                device_id_type=MESH,
            ).start()

        to_all(one)

    def band_scale(which, recv):
        pltpu.make_async_copy(recv, recv, st_recv.at[which]).wait()
        stat_send[4 + which, 0:2, :] = stat_send[which, 0:2, :] + jnp.sum(recv[...], axis=0)
        total = all_groups(stat_send[4 + which], REG // 32)
        return scale_shift(
            total[0:1], total[1:2], float(BAND_ROWS * BAND_COLS * (REG // 32))
        )

    def send_patch(which, s, q, recv):
        s = jnp.sum(s, axis=0, keepdims=True)
        q = jnp.sum(q, axis=0, keepdims=True)
        stat_send[which, 0:1, :] = s[:, :128]
        stat_send[which, 1:2, :] = s[:, 128:]
        stat_send[which, 2:3, :] = q[:, :128]
        stat_send[which, 3:4, :] = q[:, 128:]
        for step in range(1, LAT):
            pltpu.make_async_remote_copy(
                src_ref=stat_send.at[which, pl.ds(0, 4)],
                dst_ref=recv.at[step - 1],
                send_sem=st_send.at[which],
                recv_sem=st_recv.at[which],
                device_id={"lat": lax.rem(lat + step, LAT)},
                device_id_type=MESH,
            ).start()

    def patch_scale(which, recv):
        pltpu.make_async_copy(recv, recv, st_recv.at[which]).wait()
        stat_send[4 + which, 0:4, :] = stat_send[which, 0:4, :] + jnp.sum(recv[...], axis=0)
        total = all_groups(stat_send[4 + which], DIF // 32)
        sums = jnp.concatenate([total[0:1], total[1:2]], axis=1)
        squares = jnp.concatenate([total[2:3], total[3:4]], axis=1)
        return scale_shift(sums, squares, float(BAND_ROWS * PATCH * (DIF // 32)))

    stats = [first_rows(1, 3, 6), first_rows(2, 2, 4), first_rows(3, 0, 3)]
    stat_send[...] = jnp.zeros_like(stat_send)
    send_band(0, sum(s for s, _ in stats), sum(q for _, q in stats), stat_one)

    put_window(0)
    put_window(4)
    first_rows(0, 0, 6)
    first_rows(1, 2, 3)
    first_rows(3, 3, 6)
    first_rows(4, 2, 6)
    own_xt = xt_far[OFF : OFF + PATCH, :256]
    put_part(1, own_xt)

    def patch_rows(win):
        return ((3, 6), (2, 4), (0, 3))[win]

    def rest_rows(win):
        return ((0, 3), None, (3, 6))[win]

    for win in range(3):
        for span in (patch_rows(win), rest_rows(win)):
            if span is None:
                continue
            low, high = span
            out = jnp.dot(
                parts[win, :, 0:768],
                wb_patch[0:768, low * DIF : high * DIF],
                preferred_element_type=F32,
            )
            for p in range(low, high):
                e = win * 4 + 5 + p
                partial[(e - 5) * PATCH : (e - 4) * PATCH, :] = out[
                    :, (p - low) * DIF : (p - low + 1) * DIF
                ]

    def activate_band(source, a, b, e):
        ok = row_ok(e)
        at = at_row(e, W)
        half = source[pl.ds(at, W), :].astype(F32) * (a * ok) + b * ok
        out = half_silu(half)
        act[0, pl.ds(at, W), :] = pltpu.roll(out, 1, axis=0).astype(BF16)
        act[1, pl.ds(at, W), :] = out.astype(BF16)
        act[2, pl.ds(at, W), :] = pltpu.roll(out, W - 1, axis=0).astype(BF16)

    def loop(count, body):
        lax.fori_loop(0, count, lambda i, c: (body(i), c)[1], 0)

    def conv_band(weight, e, pairs):
        def rows_of(q, dx):
            return [
                act[dx, pl.ds(at_row(e + 2 * k + q - 1, W), W), :] for k in range(pairs)
            ]

        lhs = jnp.concatenate(
            [
                jnp.concatenate(rows_of(q, dx), axis=0)
                for q in range(4)
                for dx in range(3)
            ],
            axis=1,
        )
        out = jnp.dot(lhs, weight[...], preferred_element_type=F32)
        return [
            out[(r // 2) * W : (r // 2 + 1) * W, (r % 2) * REG : (r % 2 + 1) * REG]
            for r in range(2 * pairs)
        ]

    a, b = band_scale(0, stat_one)
    for load in loads[0]:
        load.wait()
    s = jnp.zeros((8, REG), F32)
    q = jnp.zeros((8, REG), F32)
    ready = 7
    for e, pairs in SECOND_GROUPS:
        while ready <= e + 2 * pairs:
            activate_band(first, a, b, ready)
            ready += 1
        for i, out in enumerate(conv_band(w_one, e, pairs)):
            out = out.astype(BF16)
            second[(e + i) * W : (e + i + 1) * W, :] = out
            cell = out[SIDE : SIDE + COLS].astype(F32)
            s = s + fold(cell)
            q = q + fold(cell * cell)
    send_band(1, s, q, stat_two)

    def second_rest(i):
        e = 2 + i * 14
        for k, out in enumerate(conv_band(w_one, e, 3)):
            second[pl.ds(at_row(e + k, W), W), :] = out.astype(BF16)

    loop(12, lambda i: activate_band(first, a, b, 1 + i + (i // 6) * 10))
    loop(2, second_rest)

    a2, b2 = band_scale(1, stat_two)
    for load in loads[1]:
        load.wait()

    def third_rows(e, pairs):
        for k, out in enumerate(conv_band(w_two, e, pairs)):
            at = at_row(e + k, W)
            out = first[pl.ds(at, W), :].astype(F32) + out
            third[pl.ds(at, W), :] = (out * row_ok(e + k)).astype(BF16)

    ready = 5
    for e, pairs in THIRD_GROUPS:
        while ready <= e + 2 * pairs:
            activate_band(second, a2, b2, ready)
            ready += 1
        third_rows(e, pairs)

    def mean_terms(low, high):
        lhs = jnp.concatenate([third[e * W : (e + 1) * W, :] for e in range(low, high)], axis=1)
        return [
            jnp.dot(
                lhs,
                wb_mean[(low - 3) * REG : (high - 3) * REG, dx * 256 : (dx + 1) * 256],
                preferred_element_type=F32,
            )
            for dx in range(3)
        ]

    def put_mean():
        total = (
            pltpu.roll(mean_acc[0], 1, axis=0)
            + mean_acc[1]
            + pltpu.roll(mean_acc[2], W - 1, axis=0)
        )[OFF : OFF + PATCH]
        put_part(2, total * lane_ok)
        return total

    def patch_first_rows(win, span):
        low, high = span
        out = jnp.dot(
            parts[win, :, 768:1152],
            wb_patch[768:1152, low * DIF : high * DIF],
            preferred_element_type=F32,
        )
        s = jnp.zeros((8, DIF), F32)
        q = jnp.zeros((8, DIF), F32)
        for p in range(low, high):
            e = win * 4 + 5 + p
            at = (e - 5) * PATCH
            row = out[:, (p - low) * DIF : (p - low + 1) * DIF] + partial[at : at + PATCH, :]
            row = row.astype(BF16)
            p_first[at : at + PATCH, :] = row
            if 8 <= e < 16:
                cell = row.astype(F32)
                s = s + fold(cell)
                q = q + fold(cell * cell)
        return s, q

    for dx, term in enumerate(mean_terms(6, 18)):
        mean_acc[dx] = term
    put_mean()
    stats = [patch_first_rows(win, patch_rows(win)) for win in range(3)]
    send_patch(2, sum(s for s, _ in stats), sum(q for _, q in stats), stat_three)

    def activate_rest(i):
        activate_band(second, a2, b2, 2 + i + (i // 3) * 14)

    loop(6, activate_rest)
    loop(2, lambda i: third_rows(3 + 14 * i, 2))
    for low, high in ((3, 6), (18, 21)):
        for dx, term in enumerate(mean_terms(low, high)):
            mean_acc[dx] = mean_acc[dx] + term
    mean_all = put_mean()
    mean_own = pltpu.roll(mean_all, 192, axis=1)[:, :128]
    noise_own = pltpu.roll(noise_keep[...], 192, axis=1)[:, :128]
    base = mean_own + noise_own

    def put_out(out_ref, values):
        flat = pltpu.roll(values.T, PATCH - MARGIN, axis=1)[:, :COLS]
        for r in range(ROWS):
            out_ref[:, r, :] = flat[r * CH : r * CH + OUTC, :]

    put_out(mean_out, mean_own)
    pad32[...] = base
    patch_first_rows(0, rest_rows(0))
    patch_first_rows(2, rest_rows(2))

    spot16 = lax.broadcasted_iota(jnp.int32, (16, DIF), 0)

    def activate_patch(source, shift_row, a, b, e):
        ok = row_ok(e)
        half = source[pl.ds(at_row(e - shift_row, PATCH), PATCH), :].astype(F32) * (a * ok) + b * ok
        out = half_silu(half)
        at = at_row(e - 5, PATCH)
        later = pltpu.roll(out, 1, axis=0)
        sooner = pltpu.roll(out, PATCH - 1, axis=0)
        p_act[0, pl.ds(at, 16), :] = jnp.where(spot16 == 0, 0.0, later[:16]).astype(BF16)
        p_act[0, pl.ds(at + 16, PATCH - 16), :] = later[16:].astype(BF16)
        p_act[1, pl.ds(at, PATCH), :] = out.astype(BF16)
        p_act[2, pl.ds(at, PATCH - 16), :] = sooner[:-16].astype(BF16)
        p_act[2, pl.ds(at + PATCH - 16, 16), :] = jnp.where(
            spot16 == 15, 0.0, sooner[-16:]
        ).astype(BF16)

    def conv_patch(weight, e, rows):
        lhs = jnp.concatenate(
            [
                p_act[dx, pl.ds(at_row(e + dy - 6, PATCH), rows * PATCH), :]
                for dy in range(3)
                for dx in range(3)
            ],
            axis=1,
        )
        return jnp.dot(lhs, weight[...], preferred_element_type=F32)

    a3, b3 = patch_scale(2, stat_three)
    for load in loads[2]:
        load.wait()
    s = jnp.zeros((8, DIF), F32)
    q = jnp.zeros((8, DIF), F32)
    ready = 7
    for e, rows in P_SECOND_GROUPS:
        while ready <= e + rows:
            activate_patch(p_first, 5, a3, b3, ready)
            ready += 1
        out = conv_patch(d_one, e, rows).astype(BF16)
        p_second[(e - 6) * PATCH : (e - 6 + rows) * PATCH, :] = out
        cell = out.astype(F32)
        s = s + fold(cell)
        q = q + fold(cell * cell)
    send_patch(3, s, q, stat_four)

    def p_second_rest(i):
        e = 6 + i * 10
        out = conv_patch(d_one, e, 2).astype(BF16)
        p_second[pl.ds(at_row(e - 6, PATCH), 2 * PATCH), :] = out

    loop(4, lambda i: activate_patch(p_first, 5, a3, b3, 5 + i + (i // 2) * 10))
    loop(2, p_second_rest)

    a4, b4 = patch_scale(3, stat_four)
    for load in loads[3]:
        load.wait()
    ready = 6
    for e, rows in P_THIRD_GROUPS:
        while ready <= e + rows:
            activate_patch(p_second, 6, a4, b4, ready)
            ready += 1
        conv = conv_patch(d_two, e, rows)
        for k in range(rows):
            out = p_first[(e + k - 5) * PATCH : (e + k - 4) * PATCH, :].astype(F32)
            out = (out + conv[k * PATCH : (k + 1) * PATCH]) * row_ok(e + k)
            p_third[(e + k - 7) * PATCH : (e + k - 6) * PATCH, :] = out.astype(BF16)

    lhs = jnp.concatenate([p_third[e * PATCH : (e + 1) * PATCH, :] for e in range(10)], axis=1)
    out = jnp.dot(lhs, wb_vel[...], preferred_element_type=F32)
    velocity = shift(out[:, 0:128], 0) + out[:, 128:256] + shift(out[:, 256:384], 2)
    edge_send[0] = velocity[0:MARGIN]
    edge_send[1] = velocity[PATCH - MARGIN : PATCH]
    edges = [
        pltpu.make_async_remote_copy(
            src_ref=edge_send.at[k],
            dst_ref=edge_recv.at[k],
            send_sem=e_send.at[k],
            recv_sem=e_recv.at[k],
            device_id={"lon": lax.rem(lon + LON + step, LON)},
            device_id_type=MESH,
        )
        for k, step in ((0, -1), (1, 1))
    ]
    for edge in edges:
        edge.start()
    for k in order:
        copies[k].wait_send()
    for which, recv in enumerate((stat_one, stat_two, stat_three, stat_four)):
        pltpu.make_async_copy(recv, recv, st_send.at[which]).wait()
    for edge in edges:
        edge.wait()
    from_left = velocity[MARGIN : 2 * MARGIN] + edge_recv[1]
    from_right = velocity[COLS : COLS + MARGIN] + edge_recv[0]
    total = jnp.concatenate(
        [
            velocity[0:MARGIN],
            from_left * 0.5,
            velocity[2 * MARGIN : COLS],
            from_right * 0.5,
            velocity[COLS + MARGIN :],
        ],
        axis=0,
    )
    put_out(field_out, pad32[...] + total)


def hand_over(mean_in, field_in, mean_out, field_out):
    mean_out[...] = mean_in[...]
    field_out[...] = field_in[...]


def on_device(coarse, static, noise_seeds, w_in, w_one, w_two, w_out, d_in, d_one, d_two, d_out):
    vmem = pl.BlockSpec(memory_space=pltpu.VMEM)
    smem = pl.BlockSpec(memory_space=pltpu.SMEM)
    hbm = pl.BlockSpec(memory_space=pl.ANY)
    out = jax.ShapeDtypeStruct((OUTC, ROWS, COLS), F32)
    results = pl.pallas_call(
        kernel,
        out_shape=(pltpu.VMEM((OUTC, ROWS, COLS), F32),) * 2,
        in_specs=[hbm, hbm, smem] + [hbm] * 8,
        out_specs=(vmem, vmem),
        scratch_shapes=[
            pltpu.VMEM((OUTC, ROWS, COLS), F32),
            pltpu.VMEM((CH - OUTC, ROWS, COLS), F32),
            pltpu.VMEM((9, CH, REG), BF16),
            pltpu.VMEM((9, OUTC, REG), BF16),
            pltpu.VMEM((9, 40, DIF), BF16),
            pltpu.VMEM((9, OUTC, DIF), BF16),
            pltpu.VMEM((12 * REG, 2 * REG), BF16),
            pltpu.VMEM((12 * REG, 2 * REG), BF16),
            pltpu.VMEM((9 * DIF, DIF), BF16),
            pltpu.VMEM((9 * DIF, DIF), BF16),
            pltpu.VMEM((128, 256), F32),
            pltpu.VMEM((128, 256), BF16),
            pltpu.VMEM((2, 128, 256), BF16),
            pltpu.VMEM((6, 128, 128), BF16),
            pltpu.VMEM((5, W, 384), BF16),
            pltpu.VMEM((384, 6 * REG), BF16),
            pltpu.VMEM((1152, 6 * DIF), BF16),
            pltpu.VMEM((18 * REG, 768), BF16),
            pltpu.VMEM((10 * DIF, 384), BF16),
            pltpu.VMEM((FRAME * W, REG), BF16),
            pltpu.VMEM((FRAME * W, REG), BF16),
            pltpu.VMEM((FRAME * W, REG), BF16),
            pltpu.VMEM((3, FRAME * W, REG), BF16),
            pltpu.VMEM((PATCH, 256), F32),
            pltpu.VMEM((3, PATCH, 1152), BF16),
            pltpu.VMEM((14 * PATCH, DIF), F32),
            pltpu.VMEM((3, W, 256), F32),
            pltpu.VMEM((14 * PATCH, DIF), BF16),
            pltpu.VMEM((12 * PATCH, DIF), BF16),
            pltpu.VMEM((10 * PATCH, DIF), BF16),
            pltpu.VMEM((3, 14 * PATCH, DIF), BF16),
            pltpu.VMEM((256, 128), F32),
            pltpu.VMEM((128, DIF), F32),
            pltpu.VMEM((2, MARGIN, 128), F32),
            pltpu.VMEM((2, MARGIN, 128), F32),
            pltpu.VMEM((8, 8, 128), F32),
            pltpu.VMEM((ALL - 1, 2, 128), F32),
            pltpu.VMEM((ALL - 1, 2, 128), F32),
            pltpu.VMEM((LAT - 1, 4, 128), F32),
            pltpu.VMEM((LAT - 1, 4, 128), F32),
            pltpu.SemaphoreType.DMA((12,)),
            pltpu.SemaphoreType.DMA((8,)),
            pltpu.SemaphoreType.DMA((8,)),
            pltpu.SemaphoreType.DMA((4,)),
            pltpu.SemaphoreType.DMA((4,)),
            pltpu.SemaphoreType.DMA((2,)),
            pltpu.SemaphoreType.DMA((2,)),
        ],
        compiler_params=pltpu.CompilerParams(
            collective_id=0, has_side_effects=True, vmem_limit_bytes=60 * 1024 * 1024
        ),
    )(
        coarse,
        static,
        noise_seeds,
        w_in.reshape(9, CH, REG),
        w_one.reshape(9 * REG, REG),
        w_two.reshape(9 * REG, REG),
        jnp.transpose(w_out.reshape(9, REG, OUTC), (0, 2, 1)),
        d_in.reshape(9, 40, DIF),
        d_one.reshape(9 * DIF, DIF),
        d_two.reshape(9 * DIF, DIF),
        jnp.transpose(d_out.reshape(9, DIF, OUTC), (0, 2, 1)),
    )
    return pl.pallas_call(
        hand_over,
        out_shape=(out, out),
        in_specs=[vmem, vmem],
        out_specs=(vmem, vmem),
        compiler_params=pltpu.CompilerParams(vmem_limit_bytes=4 * 1024 * 1024),
    )(*results)


def solution(mesh):
    brick = P(None, "lat", "lon")
    return jax.shard_map(
        on_device,
        mesh=mesh,
        in_specs=(brick, brick) + (P(),) * 9,
        out_specs=(brick, brick),
        check_vma=False,
    )
```

```python
import functools

import jax
import jax.numpy as jnp
from jax import lax
from jax.experimental import pallas as pl
from jax.experimental.pallas import tpu as pltpu
from jax.sharding import PartitionSpec as P

MESH = pl.DeviceIdType.MESH
F32 = jnp.float32
BF16 = jnp.bfloat16

LON, LAT = 16, 8
ALL = LON * LAT
ROWS = 8
COLS = 192
BAND_ROWS = ROWS * LAT
BAND_COLS = COLS * LON
MARGIN = 32
PATCH = COLS + 2 * MARGIN
SIDE = 40
W = COLS + 2 * SIDE
OFF = SIDE - MARGIN
FRAME = 3 * ROWS
CH = 16
REG = 128
DIF = 256
OUTC = 12
STEPS = (2, 1, 3, 0)
P_SECOND_GROUPS = ((8, 4), (12, 4))
P_THIRD_GROUPS = ((7, 4), (11, 4), (15, 2))
SECOND_GROUPS = ((8, 2), (12, 2))
THIRD_GROUPS = ((6, 2), (10, 2), (14, 2))
EPS = 1e-05

AROUND = ((0, -1), (0, 1), (-1, -1), (-1, 0), (-1, 1), (1, -1), (1, 0), (1, 1))


def hashed(value):
    for _ in range(2):
        value = value ^ (lax.shift_right_logical(value, 16))
        value = value * 73244475
    return value ^ (lax.shift_right_logical(value, 16))


def at_row(row, width):
    return row * width if isinstance(row, int) else pl.multiple_of(row * width, 16)


def all_groups(stats, size):
    lane = lax.broadcasted_iota(jnp.int32, stats.shape, 1)
    step = 1
    while step < size:
        up = pltpu.roll(stats, 128 - step, axis=1)
        down = pltpu.roll(stats, step, axis=1)
        stats = stats + jnp.where((lane // step) % 2 == 0, up, down)
        step *= 2
    return stats


def scale_shift(sums, squares, count):
    mean = sums / count
    scale = lax.rsqrt(squares / count - mean * mean + EPS)
    return 0.5 * scale, -0.5 * scale * mean


def half_silu(half):
    return half + half * jnp.tanh(half)


def fold(values):
    return jnp.sum(values.reshape(values.shape[0] // 8, 8, values.shape[1]), axis=0)


def kernel(
    coarse_hbm,
    static_hbm,
    seeds,
    w_in_hbm,
    w_one_hbm,
    w_two_hbm,
    w_out_hbm,
    d_in_hbm,
    d_one_hbm,
    d_two_hbm,
    d_out_hbm,
    mean_out,
    field_out,
    coarse,
    static,
    w_in,
    w_out,
    d_in,
    d_out,
    w_one,
    w_two,
    d_one,
    d_two,
    own32,
    own16,
    tall,
    wide,
    xw,
    wb_in,
    wb_patch,
    wb_mix,
    wb_mean,
    wb_vel,
    first,
    second,
    third,
    act,
    noise_keep,
    parts,
    mixed,
    partial,
    mean_keep,
    p_first,
    p_second,
    p_third,
    p_act,
    pad32,
    taps,
    edge_send,
    edge_recv,
    stat_send,
    stat_one,
    stat_two,
    stat_three,
    stat_four,
    w_sem,
    in_send,
    in_recv,
    st_send,
    st_recv,
    e_send,
    e_recv,
):
    lon = lax.axis_index("lon")
    lat = lax.axis_index("lat")

    core = lax.rem(lon, 2)
    y = lax.rem(lon // 2, 4)
    x = lax.rem(lat, 4)
    z = (lon // 8) * 2 + lat // 4

    def chip(dz, dy, dx):
        there = lax.rem(z + dz, 4)
        far_lon = (there // 2) * 8 + lax.rem(y + dy, 4) * 2
        return far_lon, lax.rem(there, 2) * 4 + lax.rem(x + dx, 4)

    def reach(i):
        return jnp.where(i == 0, 2, jnp.where(i == 3, 0, jnp.where(i == 1, 1, 3)))

    def to_all(action):
        def some(i, carry):
            dz, dy = reach(i // 4), reach(lax.rem(i, 4))
            for j, dx in enumerate(STEPS):
                far_lon, far_lat = chip(dz, dy, dx)
                for k in range(2):
                    target = {"lon": far_lon + (1 - core if k == 0 else core), "lat": far_lat}
                    action(target, i * 8 + j * 2 + k)
            return carry

        lax.fori_loop(0, 15, some, 0)
        for j, dx in enumerate(STEPS):
            far_lon, far_lat = chip(0, 0, dx)
            for k in range(2):
                if (j, k) != (3, 1):
                    target = {"lon": far_lon + (1 - core if k == 0 else core), "lat": far_lat}
                    action(target, 120 + j * 2 + k)

    def row_ok(e):
        row = lat * ROWS - ROWS + e
        return jnp.where((row >= 0) & (row < BAND_ROWS), 1.0, 0.0).astype(F32)

    barrier = pltpu.get_barrier_semaphore()

    to_all(
        lambda target, slot: pl.semaphore_signal(
            barrier, inc=1, device_id=target, device_id_type=MESH
        )
    )

    wide_w = ((w_one_hbm, w_one), (w_two_hbm, w_two))
    loads = []
    for i, (src, dst) in enumerate(wide_w):
        dst[3 * 384 : 4 * 384, 0:128] = jnp.zeros((384, 128), BF16)
        dst[0:384, 128:256] = jnp.zeros((384, 128), BF16)
        loads.append(
            [
                pltpu.make_async_copy(
                    src,
                    dst.at[p * 384 : p * 384 + 9 * REG, p * 128 : (p + 1) * 128],
                    w_sem.at[i * 2 + p],
                )
                for p in range(2)
            ]
        )
    loads.append([pltpu.make_async_copy(d_one_hbm, d_one, w_sem.at[4])])
    loads.append([pltpu.make_async_copy(d_two_hbm, d_two, w_sem.at[5])])
    near = [
        pltpu.make_async_copy(coarse_hbm, coarse, w_sem.at[6]),
        pltpu.make_async_copy(static_hbm, static, w_sem.at[7]),
        pltpu.make_async_copy(w_in_hbm, w_in, w_sem.at[8]),
        pltpu.make_async_copy(w_out_hbm, w_out, w_sem.at[9]),
        pltpu.make_async_copy(d_in_hbm, d_in, w_sem.at[10]),
        pltpu.make_async_copy(d_out_hbm, d_out, w_sem.at[11]),
    ]
    for load in near:
        load.start()
    for group in loads:
        for load in group:
            load.start()
    for load in near:
        load.wait()
    own32[...] = jnp.zeros_like(own32)
    for r in range(ROWS):
        own32[r * CH : r * CH + 12, 0:COLS] = coarse[:, r, :]
        own32[r * CH + 12 : r * CH + 16, 0:COLS] = static[:, r, :]
    own16[...] = own32[...].astype(BF16)

    wb_in[...] = jnp.zeros_like(wb_in)
    for p in range(6):
        for dy in range(3):
            for dx in range(3):
                at = dx * 128 + (p + dy) * CH
                wb_in[at : at + CH, p * REG : (p + 1) * REG] = w_in[dy * 3 + dx]
    wb_patch[...] = jnp.zeros_like(wb_patch)
    wb_mix[...] = jnp.zeros_like(wb_mix)
    low_rows = lax.broadcasted_iota(jnp.int32, (40, DIF), 0) < OUTC
    for dy in range(3):
        for dx in range(3):
            raw = d_in[dy * 3 + dx].astype(F32)
            pieces = (jnp.where(low_rows, raw, 0.0)[:CH].astype(BF16), raw[24:40].astype(BF16))
            mean_piece = jnp.where(low_rows, pltpu.roll(raw, 28, axis=0), 0.0)[:CH].astype(BF16)
            for p in range(2):
                at = dx * 64 + (p + dy) * CH
                wb_mix[at : at + CH, p * DIF : (p + 1) * DIF] = mean_piece
            for part, piece in enumerate(pieces):
                for p in range(6):
                    at = part * 384 + dx * 128 + (p + dy) * CH
                    wb_patch[at : at + CH, p * DIF : (p + 1) * DIF] = piece
    taps[...] = jnp.zeros_like(taps)
    lane256 = lax.broadcasted_iota(jnp.int32, (1, 256), 1)
    lane128 = lax.broadcasted_iota(jnp.int32, (1, 128), 1)
    half_lane = lane128 < 64

    def out_weights(weight, depth, bank):
        bases = []
        for dx in range(3):
            for dy in range(3):
                at = (2 - dy) * CH
                taps[at : at + OUTC, 0:depth] = weight[dy * 3 + dx].astype(F32)
            bases.append(taps[:, 0:depth].T)
        for i in range(6):
            step = ((i - 2) * CH) % 128
            zero, one, two = (pltpu.roll(base, step, axis=1) for base in bases)
            rows = slice(i * depth, (i + 1) * depth)
            one = pltpu.roll(one, 64, axis=1)
            bank[rows, 0:128] = jnp.where(half_lane, zero, one).astype(BF16)
            bank[rows, 128:256] = jnp.where(half_lane, two, 0.0).astype(BF16)

    out_weights(w_out, REG, wb_mean)
    out_weights(d_out, DIF, wb_vel)

    lane_row = lane256 // CH
    lane_ok = jnp.zeros((1, 256), F32)
    seed = jnp.zeros((1, 256), jnp.int32)
    for r in range(16):
        row = lat * ROWS - 4 + r
        here = seeds[jnp.clip(row, 0, BAND_ROWS - 1)]
        seed = jnp.where(lane_row == r, here, seed)
        lane_ok = jnp.where(lane_row == r, row_ok(4 + r), lane_ok)

    def shift(values, dx):
        count = values.shape[0]
        spot = lax.broadcasted_iota(jnp.int32, values.shape, 0)
        if dx == 0:
            return jnp.where(spot == 0, 0.0, pltpu.roll(values, 1, axis=0))
        if dx == 2:
            return jnp.where(spot == count - 1, 0.0, pltpu.roll(values, count - 1, axis=0))
        return values

    spot_low = lax.broadcasted_iota(jnp.int32, (16, 128), 0)

    def put_part(part, values):
        windows = (values[:, :128], pltpu.roll(values, 192, axis=1)[:, :128], values[:, 128:])
        for win, block in enumerate(windows):
            at = part * 384
            later = pltpu.roll(block, 1, axis=0)
            sooner = pltpu.roll(block, PATCH - 1, axis=0)
            parts[win, 0:16, at : at + 128] = jnp.where(spot_low == 0, 0.0, later[:16]).astype(BF16)
            parts[win, 16:, at : at + 128] = later[16:].astype(BF16)
            parts[win, :, at + 128 : at + 256] = block.astype(BF16)
            parts[win, :-16, at + 256 : at + 384] = sooner[:-16].astype(BF16)
            parts[win, PATCH - 16 :, at + 256 : at + 384] = jnp.where(
                spot_low == 15, 0.0, sooner[-16:]
            ).astype(BF16)

    def noise_rows(i, carry):
        at = pl.multiple_of(i * 32, 32)
        column = lon * COLS - MARGIN + at + lax.broadcasted_iota(jnp.int32, (32, 256), 0)
        column = jnp.where(column < 0, column + BAND_COLS, column)
        column = jnp.where(column >= BAND_COLS, column - BAND_COLS, column)
        channel = lax.broadcasted_iota(jnp.int32, (32, 256), 1) % CH
        start = seed ^ ((column * OUTC + channel) * 1640531527)
        total = jnp.zeros((32, 256), jnp.int32)
        for turn in range(4):
            total = total + (hashed(start + turn * 374761393) & 65535)
        uniform = total.astype(F32) * (1.0 / 65536.0) + 4.0 / 131072.0
        noise_keep[pl.ds(at, 32), :] = (uniform - 2.0) * 1.7320508075688772 * lane_ok
        return carry

    lax.fori_loop(0, PATCH // 32, noise_rows, 0)
    put_part(0, noise_keep[...])

    pl.semaphore_wait(barrier, ALL - 1)

    def around(k):
        dlon, dlat = AROUND[k]
        target = {"lon": lax.rem(lon + dlon + LON, LON), "lat": lax.rem(lat + dlat + LAT, LAT)}
        if dlon == 0:
            src, dst = own16, tall.at[k]
        elif dlon == 1:
            src, dst = own16.at[:, 128:256], wide.at[k - 2]
        else:
            src, dst = own16.at[:, 0:128], wide.at[k - 2]
        return pltpu.make_async_remote_copy(
            src_ref=src,
            dst_ref=dst,
            send_sem=in_send.at[k],
            recv_sem=in_recv.at[k],
            device_id=target,
            device_id_type=MESH,
        )

    order = (2, 4, 5, 7, 3, 6, 0, 1)
    copies = {k: around(k) for k in order}
    for k in order:
        copies[k].start()
    for k in order:
        copies[k].wait_recv()

    def assemble(centre, left, right):
        lane = lax.broadcasted_iota(jnp.int32, (128, 128), 1)
        low = pltpu.roll(left, 128 - 24, axis=1)
        one = pltpu.roll(centre[:, :128], SIDE, axis=1)
        two = pltpu.roll(centre[:, 128:], SIDE, axis=1)
        high = pltpu.roll(right, SIDE + COLS - 128, axis=1)
        return jnp.concatenate(
            [
                jnp.where(lane < SIDE, low, one),
                jnp.where(lane < SIDE, one, jnp.where(lane < SIDE + COLS - 128, two, high)),
                jnp.where(lane < W - 256, high, 0.0),
            ],
            axis=1,
        )

    up = assemble(tall[1].astype(F32), wide[7 - 2].astype(F32), wide[4 - 2].astype(F32))
    mid = assemble(own16[...].astype(F32), wide[6 - 2].astype(F32), wide[3 - 2].astype(F32))
    down = assemble(tall[0].astype(F32), wide[5 - 2].astype(F32), wide[2 - 2].astype(F32))
    up = jnp.where(lat == 0, 0.0, up)
    down = jnp.where(lat == LAT - 1, 0.0, down)
    xt = jnp.concatenate([up.T, mid.T, down.T], axis=1)[:W]
    xt_far = pltpu.roll(xt, 320, axis=1)

    def put_window(win):
        at = (win // 2) * 128
        block = (xt, xt_far)[win % 2][:, at : at + 128]
        xw[win, :, 0:128] = pltpu.roll(block, 1, axis=0).astype(BF16)
        xw[win, :, 128:256] = block.astype(BF16)
        xw[win, :, 256:384] = pltpu.roll(block, W - 1, axis=0).astype(BF16)

    for win in (1, 2, 3):
        put_window(win)

    def first_rows(win, low, high):
        out = jnp.dot(
            xw[win], wb_in[:, low * REG : high * REG], preferred_element_type=F32
        ).astype(BF16)
        s = jnp.zeros((8, REG), F32)
        q = jnp.zeros((8, REG), F32)
        for p in range(low, high):
            e = win * 4 + 1 + p
            row = out[:, (p - low) * REG : (p - low + 1) * REG]
            first[e * W : (e + 1) * W, :] = row
            if 8 <= e < 16:
                cell = row[SIDE : SIDE + COLS].astype(F32)
                s = s + fold(cell)
                q = q + fold(cell * cell)
        return s, q

    def send_band(which, s, q, recv):
        stat_send[which, 0:1, :] = jnp.sum(s, axis=0, keepdims=True)
        stat_send[which, 1:2, :] = jnp.sum(q, axis=0, keepdims=True)

        def one(target, slot):
            pltpu.make_async_remote_copy(
                src_ref=stat_send.at[which, pl.ds(0, 2)],
                dst_ref=recv.at[slot],
                send_sem=st_send.at[which],
                recv_sem=st_recv.at[which],
                device_id=target,
                device_id_type=MESH,
            ).start()

        to_all(one)

    def band_scale(which, recv):
        pltpu.make_async_copy(recv, recv, st_recv.at[which]).wait()
        stat_send[4 + which, 0:2, :] = stat_send[which, 0:2, :] + jnp.sum(recv[...], axis=0)
        total = all_groups(stat_send[4 + which], REG // 32)
        return scale_shift(
            total[0:1], total[1:2], float(BAND_ROWS * BAND_COLS * (REG // 32))
        )

    def send_patch(which, s, q, recv):
        s = jnp.sum(s, axis=0, keepdims=True)
        q = jnp.sum(q, axis=0, keepdims=True)
        stat_send[which, 0:1, :] = s[:, :128]
        stat_send[which, 1:2, :] = s[:, 128:]
        stat_send[which, 2:3, :] = q[:, :128]
        stat_send[which, 3:4, :] = q[:, 128:]
        for step in range(1, LAT):
            pltpu.make_async_remote_copy(
                src_ref=stat_send.at[which, pl.ds(0, 4)],
                dst_ref=recv.at[step - 1],
                send_sem=st_send.at[which],
                recv_sem=st_recv.at[which],
                device_id={"lat": lax.rem(lat + step, LAT)},
                device_id_type=MESH,
            ).start()

    def patch_scale(which, recv):
        pltpu.make_async_copy(recv, recv, st_recv.at[which]).wait()
        stat_send[4 + which, 0:4, :] = stat_send[which, 0:4, :] + jnp.sum(recv[...], axis=0)
        total = all_groups(stat_send[4 + which], DIF // 32)
        sums = jnp.concatenate([total[0:1], total[1:2]], axis=1)
        squares = jnp.concatenate([total[2:3], total[3:4]], axis=1)
        return scale_shift(sums, squares, float(BAND_ROWS * PATCH * (DIF // 32)))

    stats = [first_rows(1, 3, 6), first_rows(2, 2, 4), first_rows(3, 0, 3)]
    stat_send[...] = jnp.zeros_like(stat_send)
    send_band(0, sum(s for s, _ in stats), sum(q for _, q in stats), stat_one)

    put_window(0)
    put_window(4)
    first_rows(0, 0, 6)
    first_rows(1, 2, 3)
    first_rows(3, 3, 6)
    first_rows(4, 2, 6)
    own_xt = xt_far[OFF : OFF + PATCH, :256]
    put_part(1, own_xt)

    def patch_rows(win):
        return ((3, 6), (2, 4), (0, 3))[win]

    def rest_rows(win):
        return ((0, 3), None, (3, 6))[win]

    for win in range(3):
        for span in (patch_rows(win), rest_rows(win)):
            if span is None:
                continue
            low, high = span
            out = jnp.dot(
                parts[win, :, 0:768],
                wb_patch[0:768, low * DIF : high * DIF],
                preferred_element_type=F32,
            )
            for p in range(low, high):
                e = win * 4 + 5 + p
                partial[(e - 5) * PATCH : (e - 4) * PATCH, :] = out[
                    :, (p - low) * DIF : (p - low + 1) * DIF
                ]

    def activate_band(source, a, b, e):
        ok = row_ok(e)
        at = at_row(e, W)
        half = source[pl.ds(at, W), :].astype(F32) * (a * ok) + b * ok
        out = half_silu(half)
        act[0, pl.ds(at, W), :] = pltpu.roll(out, 1, axis=0).astype(BF16)
        act[1, pl.ds(at, W), :] = out.astype(BF16)
        act[2, pl.ds(at, W), :] = pltpu.roll(out, W - 1, axis=0).astype(BF16)

    def loop(count, body):
        lax.fori_loop(0, count, lambda i, c: (body(i), c)[1], 0)

    def conv_band(weight, e, pairs):
        def rows_of(q, dx):
            return [
                act[dx, pl.ds(at_row(e + 2 * k + q - 1, W), W), :] for k in range(pairs)
            ]

        lhs = jnp.concatenate(
            [
                jnp.concatenate(rows_of(q, dx), axis=0)
                for q in range(4)
                for dx in range(3)
            ],
            axis=1,
        )
        out = jnp.dot(lhs, weight[...], preferred_element_type=F32)
        return [
            out[(r // 2) * W : (r // 2 + 1) * W, (r % 2) * REG : (r % 2 + 1) * REG]
            for r in range(2 * pairs)
        ]

    a, b = band_scale(0, stat_one)
    for load in loads[0]:
        load.wait()
    s = jnp.zeros((8, REG), F32)
    q = jnp.zeros((8, REG), F32)
    ready = 7
    for e, pairs in SECOND_GROUPS:
        while ready <= e + 2 * pairs:
            activate_band(first, a, b, ready)
            ready += 1
        for i, out in enumerate(conv_band(w_one, e, pairs)):
            out = out.astype(BF16)
            second[(e + i) * W : (e + i + 1) * W, :] = out
            cell = out[SIDE : SIDE + COLS].astype(F32)
            s = s + fold(cell)
            q = q + fold(cell * cell)
    send_band(1, s, q, stat_two)

    def second_rest(i):
        e = 2 + i * 14
        for k, out in enumerate(conv_band(w_one, e, 3)):
            second[pl.ds(at_row(e + k, W), W), :] = out.astype(BF16)

    loop(12, lambda i: activate_band(first, a, b, 1 + i + (i // 6) * 10))
    loop(2, second_rest)

    a2, b2 = band_scale(1, stat_two)
    for load in loads[1]:
        load.wait()

    def third_rows(e, pairs):
        for k, out in enumerate(conv_band(w_two, e, pairs)):
            at = at_row(e + k, W)
            out = first[pl.ds(at, W), :].astype(F32) + out
            third[pl.ds(at, W), :] = (out * row_ok(e + k)).astype(BF16)

    ready = 5
    for e, pairs in THIRD_GROUPS:
        while ready <= e + 2 * pairs:
            activate_band(second, a2, b2, ready)
            ready += 1
        third_rows(e, pairs)

    def mean_windows(starts):
        lhs = jnp.concatenate(
            [
                jnp.concatenate([third[(e + i - 1) * W : (e + i) * W, :] for e in starts], axis=0)
                for i in range(6)
            ],
            axis=1,
        )
        out = jnp.dot(lhs, wb_mean[...], preferred_element_type=F32)
        windows = []
        for k, e in enumerate(starts):
            low, high = out[k * W : (k + 1) * W, 0:128], out[k * W : (k + 1) * W, 128:256]
            mean = (
                pltpu.roll(low, 1, axis=0)
                + pltpu.roll(low, 64, axis=1)
                + pltpu.roll(high, W - 1, axis=0)
            )
            ok = jnp.zeros((1, 128), F32)
            for q in range(4):
                ok = jnp.where(lane128 // CH == q, row_ok(e + q), ok)
            windows.append(mean[OFF : OFF + PATCH] * ok)
        return windows

    def put_mixed(windows):
        for k, mean in enumerate(windows):
            at = k * PATCH
            later = pltpu.roll(mean, 1, axis=0)
            sooner = pltpu.roll(mean, PATCH - 1, axis=0)
            low = jnp.where(half_lane, later, pltpu.roll(mean, 64, axis=1))
            head = jnp.where((spot_low == 0) & half_lane, 0.0, low[:16])
            tail = jnp.where(spot_low == 15, 0.0, sooner[-16:])
            mixed[at : at + 16, 0:128] = head.astype(BF16)
            mixed[at + 16 : at + PATCH, 0:128] = low[16:].astype(BF16)
            mixed[at : at + PATCH - 16, 128:256] = sooner[:-16].astype(BF16)
            mixed[at + PATCH - 16 : at + PATCH, 128:256] = tail.astype(BF16)

    def patch_first_rows(starts, skip):
        out = jnp.dot(mixed[...], wb_mix[...], preferred_element_type=F32)
        s = jnp.zeros((8, DIF), F32)
        q = jnp.zeros((8, DIF), F32)
        for k, start in enumerate(starts):
            for p in range(2):
                e = start + 1 + p
                if (k, p) in skip:
                    continue
                at = (e - 5) * PATCH
                row = out[k * PATCH : (k + 1) * PATCH, p * DIF : (p + 1) * DIF]
                row = (row + partial[at : at + PATCH, :]).astype(BF16)
                p_first[at : at + PATCH, :] = row
                if 8 <= e < 16:
                    cell = row.astype(F32)
                    s = s + fold(cell)
                    q = q + fold(cell * cell)
        return s, q

    windows = mean_windows((7, 9, 11, 13))
    put_mixed(windows)
    for k, mean in enumerate(windows):
        mean_keep[k] = mean
    s, q = patch_first_rows((7, 9, 11, 13), ())
    send_patch(2, s, q, stat_three)

    def activate_rest(i):
        activate_band(second, a2, b2, 2 + i + (i // 3) * 14)

    loop(6, activate_rest)
    loop(2, lambda i: third_rows(3 + 14 * i, 2))
    put_mixed(mean_windows((4, 6, 15, 16)))
    patch_first_rows((4, 6, 15, 16), ((1, 1), (3, 0)))
    mean_own = jnp.zeros((PATCH, 128), F32)
    for k in range(4):
        here = lane128 // 32 == k
        mean_own = jnp.where(here, pltpu.roll(mean_keep[k], (32 * k - CH) % 128, axis=1), mean_own)
    noise_own = pltpu.roll(noise_keep[...], 192, axis=1)[:, :128]
    base = mean_own + noise_own

    def put_out(out_ref, values):
        flat = pltpu.roll(values.T, PATCH - MARGIN, axis=1)[:, :COLS]
        for r in range(ROWS):
            out_ref[:, r, :] = flat[r * CH : r * CH + OUTC, :]

    put_out(mean_out, mean_own)
    pad32[...] = base

    spot16 = lax.broadcasted_iota(jnp.int32, (16, DIF), 0)

    def activate_patch(source, shift_row, a, b, e):
        ok = row_ok(e)
        half = source[pl.ds(at_row(e - shift_row, PATCH), PATCH), :].astype(F32) * (a * ok) + b * ok
        out = half_silu(half)
        at = at_row(e - 5, PATCH)
        later = pltpu.roll(out, 1, axis=0)
        sooner = pltpu.roll(out, PATCH - 1, axis=0)
        p_act[0, pl.ds(at, 16), :] = jnp.where(spot16 == 0, 0.0, later[:16]).astype(BF16)
        p_act[0, pl.ds(at + 16, PATCH - 16), :] = later[16:].astype(BF16)
        p_act[1, pl.ds(at, PATCH), :] = out.astype(BF16)
        p_act[2, pl.ds(at, PATCH - 16), :] = sooner[:-16].astype(BF16)
        p_act[2, pl.ds(at + PATCH - 16, 16), :] = jnp.where(
            spot16 == 15, 0.0, sooner[-16:]
        ).astype(BF16)

    def conv_patch(weight, e, rows):
        lhs = jnp.concatenate(
            [
                p_act[dx, pl.ds(at_row(e + dy - 6, PATCH), rows * PATCH), :]
                for dy in range(3)
                for dx in range(3)
            ],
            axis=1,
        )
        return jnp.dot(lhs, weight[...], preferred_element_type=F32)

    a3, b3 = patch_scale(2, stat_three)
    for load in loads[2]:
        load.wait()
    s = jnp.zeros((8, DIF), F32)
    q = jnp.zeros((8, DIF), F32)
    ready = 7
    for e, rows in P_SECOND_GROUPS:
        while ready <= e + rows:
            activate_patch(p_first, 5, a3, b3, ready)
            ready += 1
        out = conv_patch(d_one, e, rows).astype(BF16)
        p_second[(e - 6) * PATCH : (e - 6 + rows) * PATCH, :] = out
        cell = out.astype(F32)
        s = s + fold(cell)
        q = q + fold(cell * cell)
    send_patch(3, s, q, stat_four)

    def p_second_rest(i):
        e = 6 + i * 10
        out = conv_patch(d_one, e, 2).astype(BF16)
        p_second[pl.ds(at_row(e - 6, PATCH), 2 * PATCH), :] = out

    loop(4, lambda i: activate_patch(p_first, 5, a3, b3, 5 + i + (i // 2) * 10))
    loop(2, p_second_rest)

    a4, b4 = patch_scale(3, stat_four)
    for load in loads[3]:
        load.wait()
    ready = 6
    for e, rows in P_THIRD_GROUPS:
        while ready <= e + rows:
            activate_patch(p_second, 6, a4, b4, ready)
            ready += 1
        conv = conv_patch(d_two, e, rows)
        for k in range(rows):
            out = p_first[(e + k - 5) * PATCH : (e + k - 4) * PATCH, :].astype(F32)
            out = (out + conv[k * PATCH : (k + 1) * PATCH]) * row_ok(e + k)
            p_third[(e + k - 7) * PATCH : (e + k - 6) * PATCH, :] = out.astype(BF16)

    lhs = jnp.concatenate(
        [
            jnp.concatenate([p_third[r * PATCH : (r + 1) * PATCH, :] for r in (i, i + 4)], axis=0)
            for i in range(6)
        ],
        axis=1,
    )
    out = jnp.dot(lhs, wb_vel[...], preferred_element_type=F32)

    def of_window(k):
        low, high = out[k * PATCH : (k + 1) * PATCH, :128], out[k * PATCH : (k + 1) * PATCH, 128:]
        return shift(low, 0) + pltpu.roll(low, 64, axis=1) + shift(high, 2)

    velocity = jnp.where(half_lane, of_window(0), pltpu.roll(of_window(1), 64, axis=1))
    edge_send[0] = velocity[0:MARGIN]
    edge_send[1] = velocity[PATCH - MARGIN : PATCH]
    edges = [
        pltpu.make_async_remote_copy(
            src_ref=edge_send.at[k],
            dst_ref=edge_recv.at[k],
            send_sem=e_send.at[k],
            recv_sem=e_recv.at[k],
            device_id={"lon": lax.rem(lon + LON + step, LON)},
            device_id_type=MESH,
        )
        for k, step in ((0, -1), (1, 1))
    ]
    for edge in edges:
        edge.start()
    for k in order:
        copies[k].wait_send()
    for which, recv in enumerate((stat_one, stat_two, stat_three, stat_four)):
        pltpu.make_async_copy(recv, recv, st_send.at[which]).wait()
    for edge in edges:
        edge.wait()
    from_left = velocity[MARGIN : 2 * MARGIN] + edge_recv[1]
    from_right = velocity[COLS : COLS + MARGIN] + edge_recv[0]
    total = jnp.concatenate(
        [
            velocity[0:MARGIN],
            from_left * 0.5,
            velocity[2 * MARGIN : COLS],
            from_right * 0.5,
            velocity[COLS + MARGIN :],
        ],
        axis=0,
    )
    put_out(field_out, pad32[...] + total)


def hand_over(mean_in, field_in, mean_out, field_out):
    mean_out[...] = mean_in[...]
    field_out[...] = field_in[...]


def on_device(coarse, static, noise_seeds, w_in, w_one, w_two, w_out, d_in, d_one, d_two, d_out):
    vmem = pl.BlockSpec(memory_space=pltpu.VMEM)
    smem = pl.BlockSpec(memory_space=pltpu.SMEM)
    hbm = pl.BlockSpec(memory_space=pl.ANY)
    out = jax.ShapeDtypeStruct((OUTC, ROWS, COLS), F32)
    results = pl.pallas_call(
        kernel,
        out_shape=(pltpu.VMEM((OUTC, ROWS, COLS), F32),) * 2,
        in_specs=[hbm, hbm, smem] + [hbm] * 8,
        out_specs=(vmem, vmem),
        scratch_shapes=[
            pltpu.VMEM((OUTC, ROWS, COLS), F32),
            pltpu.VMEM((CH - OUTC, ROWS, COLS), F32),
            pltpu.VMEM((9, CH, REG), BF16),
            pltpu.VMEM((9, OUTC, REG), BF16),
            pltpu.VMEM((9, 40, DIF), BF16),
            pltpu.VMEM((9, OUTC, DIF), BF16),
            pltpu.VMEM((12 * REG, 2 * REG), BF16),
            pltpu.VMEM((12 * REG, 2 * REG), BF16),
            pltpu.VMEM((9 * DIF, DIF), BF16),
            pltpu.VMEM((9 * DIF, DIF), BF16),
            pltpu.VMEM((128, 256), F32),
            pltpu.VMEM((128, 256), BF16),
            pltpu.VMEM((2, 128, 256), BF16),
            pltpu.VMEM((6, 128, 128), BF16),
            pltpu.VMEM((5, W, 384), BF16),
            pltpu.VMEM((384, 6 * REG), BF16),
            pltpu.VMEM((768, 6 * DIF), BF16),
            pltpu.VMEM((256, 2 * DIF), BF16),
            pltpu.VMEM((6 * REG, 256), BF16),
            pltpu.VMEM((6 * DIF, 256), BF16),
            pltpu.VMEM((FRAME * W, REG), BF16),
            pltpu.VMEM((FRAME * W, REG), BF16),
            pltpu.VMEM((FRAME * W, REG), BF16),
            pltpu.VMEM((3, FRAME * W, REG), BF16),
            pltpu.VMEM((PATCH, 256), F32),
            pltpu.VMEM((3, PATCH, 768), BF16),
            pltpu.VMEM((4 * PATCH, 256), BF16),
            pltpu.VMEM((14 * PATCH, DIF), F32),
            pltpu.VMEM((4, PATCH, 128), F32),
            pltpu.VMEM((14 * PATCH, DIF), BF16),
            pltpu.VMEM((12 * PATCH, DIF), BF16),
            pltpu.VMEM((10 * PATCH, DIF), BF16),
            pltpu.VMEM((3, 14 * PATCH, DIF), BF16),
            pltpu.VMEM((256, 128), F32),
            pltpu.VMEM((128, DIF), F32),
            pltpu.VMEM((2, MARGIN, 128), F32),
            pltpu.VMEM((2, MARGIN, 128), F32),
            pltpu.VMEM((8, 8, 128), F32),
            pltpu.VMEM((ALL - 1, 2, 128), F32),
            pltpu.VMEM((ALL - 1, 2, 128), F32),
            pltpu.VMEM((LAT - 1, 4, 128), F32),
            pltpu.VMEM((LAT - 1, 4, 128), F32),
            pltpu.SemaphoreType.DMA((12,)),
            pltpu.SemaphoreType.DMA((8,)),
            pltpu.SemaphoreType.DMA((8,)),
            pltpu.SemaphoreType.DMA((4,)),
            pltpu.SemaphoreType.DMA((4,)),
            pltpu.SemaphoreType.DMA((2,)),
            pltpu.SemaphoreType.DMA((2,)),
        ],
        compiler_params=pltpu.CompilerParams(
            collective_id=0, has_side_effects=True, vmem_limit_bytes=60 * 1024 * 1024
        ),
    )(
        coarse,
        static,
        noise_seeds,
        w_in.reshape(9, CH, REG),
        w_one.reshape(9 * REG, REG),
        w_two.reshape(9 * REG, REG),
        jnp.transpose(w_out.reshape(9, REG, OUTC), (0, 2, 1)),
        d_in.reshape(9, 40, DIF),
        d_one.reshape(9 * DIF, DIF),
        d_two.reshape(9 * DIF, DIF),
        jnp.transpose(d_out.reshape(9, DIF, OUTC), (0, 2, 1)),
    )
    return pl.pallas_call(
        hand_over,
        out_shape=(out, out),
        in_specs=[vmem, vmem],
        out_specs=(vmem, vmem),
        compiler_params=pltpu.CompilerParams(vmem_limit_bytes=4 * 1024 * 1024),
    )(*results)


def solution(mesh):
    brick = P(None, "lat", "lon")
    return jax.shard_map(
        on_device,
        mesh=mesh,
        in_specs=(brick, brick) + (P(),) * 9,
        out_specs=(brick, brick),
        check_vma=False,
    )
```

```python
import functools

import jax
import jax.numpy as jnp
from jax import lax
from jax.experimental import pallas as pl
from jax.experimental.pallas import tpu as pltpu
from jax.sharding import PartitionSpec as P

MESH = pl.DeviceIdType.MESH
F32 = jnp.float32
BF16 = jnp.bfloat16

LON, LAT = 16, 8
ALL = LON * LAT
ROWS = 8
COLS = 192
BAND_ROWS = ROWS * LAT
BAND_COLS = COLS * LON
MARGIN = 32
PATCH = COLS + 2 * MARGIN
SIDE = 40
W = COLS + 2 * SIDE
OFF = SIDE - MARGIN
FRAME = 3 * ROWS
CH = 16
REG = 128
DIF = 256
OUTC = 12
STEPS = (2, 1, 3, 0)
P_SECOND_GROUPS = ((8, 4), (12, 4))
P_THIRD_GROUPS = ((7, 4), (11, 4), (15, 2))
SECOND_GROUPS = ((8, 2), (12, 2))
THIRD_GROUPS = ((6, 2), (10, 2), (14, 2))
EPS = 1e-05

AROUND = ((0, -1), (0, 1), (-1, -1), (-1, 0), (-1, 1), (1, -1), (1, 0), (1, 1))


def hashed(value):
    for _ in range(2):
        value = value ^ (lax.shift_right_logical(value, 16))
        value = value * 73244475
    return value ^ (lax.shift_right_logical(value, 16))


def at_row(row, width):
    return row * width if isinstance(row, int) else pl.multiple_of(row * width, 16)


def all_groups(stats, size):
    lane = lax.broadcasted_iota(jnp.int32, stats.shape, 1)
    step = 1
    while step < size:
        up = pltpu.roll(stats, 128 - step, axis=1)
        down = pltpu.roll(stats, step, axis=1)
        stats = stats + jnp.where((lane // step) % 2 == 0, up, down)
        step *= 2
    return stats


def scale_shift(sums, squares, count):
    mean = sums / count
    scale = lax.rsqrt(squares / count - mean * mean + EPS)
    return 0.5 * scale, -0.5 * scale * mean


def half_silu(half):
    return half + half * jnp.tanh(half)


def fold(values):
    return jnp.sum(values.reshape(values.shape[0] // 8, 8, values.shape[1]), axis=0)


def kernel(
    coarse_hbm,
    static_hbm,
    seeds,
    w_in_hbm,
    w_one_hbm,
    w_two_hbm,
    w_out_hbm,
    d_in_hbm,
    d_one_hbm,
    d_two_hbm,
    d_out_hbm,
    mean_out,
    field_out,
    coarse,
    static,
    w_in,
    w_out,
    d_in,
    d_out,
    w_one,
    w_two,
    d_one,
    d_two,
    own32,
    own16,
    tall,
    wide,
    xw,
    wb_in,
    wb_patch,
    wb_mix,
    wb_mean,
    wb_vel,
    first,
    second,
    third,
    act,
    noise_keep,
    parts,
    mixed,
    partial,
    mean_keep,
    p_first,
    p_second,
    p_third,
    p_act,
    pad32,
    taps,
    edge_send,
    edge_recv,
    stat_send,
    stat_one,
    stat_two,
    stat_three,
    stat_four,
    w_sem,
    in_send,
    in_recv,
    st_send,
    st_recv,
    e_send,
    e_recv,
):
    lon = lax.axis_index("lon")
    lat = lax.axis_index("lat")

    core = lax.rem(lon, 2)
    y = lax.rem(lon // 2, 4)
    x = lax.rem(lat, 4)
    z = (lon // 8) * 2 + lat // 4

    def chip(dz, dy, dx):
        there = lax.rem(z + dz, 4)
        far_lon = (there // 2) * 8 + lax.rem(y + dy, 4) * 2
        return far_lon, lax.rem(there, 2) * 4 + lax.rem(x + dx, 4)

    def reach(i):
        return jnp.where(i == 0, 2, jnp.where(i == 3, 0, jnp.where(i == 1, 1, 3)))

    def to_all(action):
        def some(i, carry):
            dz, dy = reach(i // 4), reach(lax.rem(i, 4))
            for j, dx in enumerate(STEPS):
                far_lon, far_lat = chip(dz, dy, dx)
                for k in range(2):
                    target = {"lon": far_lon + (1 - core if k == 0 else core), "lat": far_lat}
                    action(target, i * 8 + j * 2 + k)
            return carry

        lax.fori_loop(0, 15, some, 0)
        for j, dx in enumerate(STEPS):
            far_lon, far_lat = chip(0, 0, dx)
            for k in range(2):
                if (j, k) != (3, 1):
                    target = {"lon": far_lon + (1 - core if k == 0 else core), "lat": far_lat}
                    action(target, 120 + j * 2 + k)

    def row_ok(e):
        row = lat * ROWS - ROWS + e
        return jnp.where((row >= 0) & (row < BAND_ROWS), 1.0, 0.0).astype(F32)

    barrier = pltpu.get_barrier_semaphore()

    to_all(
        lambda target, slot: pl.semaphore_signal(
            barrier, inc=1, device_id=target, device_id_type=MESH
        )
    )

    wide_w = ((w_one_hbm, w_one), (w_two_hbm, w_two))
    loads = []
    for i, (src, dst) in enumerate(wide_w):
        dst[3 * 384 : 4 * 384, 0:128] = jnp.zeros((384, 128), BF16)
        dst[0:384, 128:256] = jnp.zeros((384, 128), BF16)
        loads.append(
            [
                pltpu.make_async_copy(
                    src,
                    dst.at[p * 384 : p * 384 + 9 * REG, p * 128 : (p + 1) * 128],
                    w_sem.at[i * 2 + p],
                )
                for p in range(2)
            ]
        )
    loads.append([pltpu.make_async_copy(d_one_hbm, d_one, w_sem.at[4])])
    loads.append([pltpu.make_async_copy(d_two_hbm, d_two, w_sem.at[5])])
    near = [
        pltpu.make_async_copy(coarse_hbm, coarse, w_sem.at[6]),
        pltpu.make_async_copy(static_hbm, static, w_sem.at[7]),
        pltpu.make_async_copy(w_in_hbm, w_in, w_sem.at[8]),
        pltpu.make_async_copy(w_out_hbm, w_out, w_sem.at[9]),
        pltpu.make_async_copy(d_in_hbm, d_in, w_sem.at[10]),
        pltpu.make_async_copy(d_out_hbm, d_out, w_sem.at[11]),
    ]
    for load in near:
        load.start()
    for group in loads:
        for load in group:
            load.start()
    for load in near:
        load.wait()
    own32[...] = jnp.zeros_like(own32)
    for r in range(ROWS):
        own32[r * CH : r * CH + 12, 0:COLS] = coarse[:, r, :]
        own32[r * CH + 12 : r * CH + 16, 0:COLS] = static[:, r, :]
    own16[...] = own32[...].astype(BF16)

    wb_in[...] = jnp.zeros_like(wb_in)
    for p in range(6):
        for dy in range(3):
            for dx in range(3):
                at = dx * 128 + (p + dy) * CH
                wb_in[at : at + CH, p * REG : (p + 1) * REG] = w_in[dy * 3 + dx]
    wb_patch[...] = jnp.zeros_like(wb_patch)
    wb_mix[...] = jnp.zeros_like(wb_mix)
    low_rows = lax.broadcasted_iota(jnp.int32, (40, DIF), 0) < OUTC
    for dy in range(3):
        for dx in range(3):
            raw = d_in[dy * 3 + dx].astype(F32)
            pieces = (jnp.where(low_rows, raw, 0.0)[:CH].astype(BF16), raw[24:40].astype(BF16))
            mean_piece = jnp.where(low_rows, pltpu.roll(raw, 28, axis=0), 0.0)[:CH].astype(BF16)
            for p in range(2):
                at = dx * 64 + (p + dy) * CH
                wb_mix[at : at + CH, p * DIF : (p + 1) * DIF] = mean_piece
            for part, piece in enumerate(pieces):
                for p in range(6):
                    at = part * 384 + dx * 128 + (p + dy) * CH
                    wb_patch[at : at + CH, p * DIF : (p + 1) * DIF] = piece
    taps[...] = jnp.zeros_like(taps)
    lane256 = lax.broadcasted_iota(jnp.int32, (1, 256), 1)
    lane128 = lax.broadcasted_iota(jnp.int32, (1, 128), 1)
    half_lane = lane128 < 64

    def out_weights(weight, depth, bank):
        bases = []
        for dx in range(3):
            for dy in range(3):
                at = (2 - dy) * CH
                taps[at : at + OUTC, 0:depth] = weight[dy * 3 + dx].astype(F32)
            bases.append(taps[:, 0:depth].T)
        for i in range(6):
            step = ((i - 2) * CH) % 128
            zero, one, two = (pltpu.roll(base, step, axis=1) for base in bases)
            rows = slice(i * depth, (i + 1) * depth)
            one = pltpu.roll(one, 64, axis=1)
            bank[rows, 0:128] = jnp.where(half_lane, zero, one).astype(BF16)
            bank[rows, 128:256] = jnp.where(half_lane, two, 0.0).astype(BF16)

    out_weights(w_out, REG, wb_mean)
    out_weights(d_out, DIF, wb_vel)

    lane_row = lane256 // CH
    lane_ok = jnp.zeros((1, 256), F32)
    seed = jnp.zeros((1, 256), jnp.int32)
    for r in range(16):
        row = lat * ROWS - 4 + r
        here = seeds[jnp.clip(row, 0, BAND_ROWS - 1)]
        seed = jnp.where(lane_row == r, here, seed)
        lane_ok = jnp.where(lane_row == r, row_ok(4 + r), lane_ok)

    def shift(values, dx):
        count = values.shape[0]
        spot = lax.broadcasted_iota(jnp.int32, values.shape, 0)
        if dx == 0:
            return jnp.where(spot == 0, 0.0, pltpu.roll(values, 1, axis=0))
        if dx == 2:
            return jnp.where(spot == count - 1, 0.0, pltpu.roll(values, count - 1, axis=0))
        return values

    spot_low = lax.broadcasted_iota(jnp.int32, (16, 128), 0)

    def put_part(part, values):
        windows = (values[:, :128], pltpu.roll(values, 192, axis=1)[:, :128], values[:, 128:])
        for win, block in enumerate(windows):
            at = part * 384
            later = pltpu.roll(block, 1, axis=0)
            sooner = pltpu.roll(block, PATCH - 1, axis=0)
            parts[win, 0:16, at : at + 128] = jnp.where(spot_low == 0, 0.0, later[:16]).astype(BF16)
            parts[win, 16:, at : at + 128] = later[16:].astype(BF16)
            parts[win, :, at + 128 : at + 256] = block.astype(BF16)
            parts[win, :-16, at + 256 : at + 384] = sooner[:-16].astype(BF16)
            parts[win, PATCH - 16 :, at + 256 : at + 384] = jnp.where(
                spot_low == 15, 0.0, sooner[-16:]
            ).astype(BF16)

    def noise_rows(i, carry):
        at = pl.multiple_of(i * 32, 32)
        column = lon * COLS - MARGIN + at + lax.broadcasted_iota(jnp.int32, (32, 256), 0)
        column = jnp.where(column < 0, column + BAND_COLS, column)
        column = jnp.where(column >= BAND_COLS, column - BAND_COLS, column)
        channel = lax.broadcasted_iota(jnp.int32, (32, 256), 1) % CH
        start = seed ^ ((column * OUTC + channel) * 1640531527)
        total = jnp.zeros((32, 256), jnp.int32)
        for turn in range(4):
            total = total + (hashed(start + turn * 374761393) & 65535)
        uniform = total.astype(F32) * (1.0 / 65536.0) + 4.0 / 131072.0
        noise_keep[pl.ds(at, 32), :] = (uniform - 2.0) * 1.7320508075688772 * lane_ok
        return carry

    lax.fori_loop(0, PATCH // 32, noise_rows, 0)
    put_part(0, noise_keep[...])

    pl.semaphore_wait(barrier, ALL - 1)

    def around(k):
        dlon, dlat = AROUND[k]
        target = {"lon": lax.rem(lon + dlon + LON, LON), "lat": lax.rem(lat + dlat + LAT, LAT)}
        if dlon == 0:
            src, dst = own16, tall.at[k]
        elif dlon == 1:
            src, dst = own16.at[:, 128:256], wide.at[k - 2]
        else:
            src, dst = own16.at[:, 0:128], wide.at[k - 2]
        return pltpu.make_async_remote_copy(
            src_ref=src,
            dst_ref=dst,
            send_sem=in_send.at[k],
            recv_sem=in_recv.at[k],
            device_id=target,
            device_id_type=MESH,
        )

    order = (2, 4, 5, 7, 3, 6, 0, 1)
    copies = {k: around(k) for k in order}
    for k in order:
        copies[k].start()
    for k in order:
        copies[k].wait_recv()

    def assemble(centre, left, right):
        lane = lax.broadcasted_iota(jnp.int32, (128, 128), 1)
        low = pltpu.roll(left, 128 - 24, axis=1)
        one = pltpu.roll(centre[:, :128], SIDE, axis=1)
        two = pltpu.roll(centre[:, 128:], SIDE, axis=1)
        high = pltpu.roll(right, SIDE + COLS - 128, axis=1)
        return jnp.concatenate(
            [
                jnp.where(lane < SIDE, low, one),
                jnp.where(lane < SIDE, one, jnp.where(lane < SIDE + COLS - 128, two, high)),
                jnp.where(lane < W - 256, high, 0.0),
            ],
            axis=1,
        )

    up = assemble(tall[1].astype(F32), wide[7 - 2].astype(F32), wide[4 - 2].astype(F32))
    mid = assemble(own16[...].astype(F32), wide[6 - 2].astype(F32), wide[3 - 2].astype(F32))
    down = assemble(tall[0].astype(F32), wide[5 - 2].astype(F32), wide[2 - 2].astype(F32))
    up = jnp.where(lat == 0, 0.0, up)
    down = jnp.where(lat == LAT - 1, 0.0, down)
    xt = jnp.concatenate([up.T, mid.T, down.T], axis=1)[:W]
    xt_far = pltpu.roll(xt, 320, axis=1)

    def put_window(win):
        at = (win // 2) * 128
        block = (xt, xt_far)[win % 2][:, at : at + 128]
        xw[win, :, 0:128] = pltpu.roll(block, 1, axis=0).astype(BF16)
        xw[win, :, 128:256] = block.astype(BF16)
        xw[win, :, 256:384] = pltpu.roll(block, W - 1, axis=0).astype(BF16)

    for win in (1, 2, 3):
        put_window(win)

    def first_rows(win, low, high):
        out = jnp.dot(
            xw[win], wb_in[:, low * REG : high * REG], preferred_element_type=F32
        ).astype(BF16)
        s = jnp.zeros((8, REG), F32)
        q = jnp.zeros((8, REG), F32)
        for p in range(low, high):
            e = win * 4 + 1 + p
            row = out[:, (p - low) * REG : (p - low + 1) * REG]
            first[e * W : (e + 1) * W, :] = row
            if 8 <= e < 16:
                cell = row[SIDE : SIDE + COLS].astype(F32)
                s = s + fold(cell)
                q = q + fold(cell * cell)
        return s, q

    def send_band(which, s, q, recv):
        stat_send[which, 0:1, :] = jnp.sum(s, axis=0, keepdims=True)
        stat_send[which, 1:2, :] = jnp.sum(q, axis=0, keepdims=True)

        def one(target, slot):
            pltpu.make_async_remote_copy(
                src_ref=stat_send.at[which, pl.ds(0, 2)],
                dst_ref=recv.at[slot],
                send_sem=st_send.at[which],
                recv_sem=st_recv.at[which],
                device_id=target,
                device_id_type=MESH,
            ).start()

        to_all(one)

    def band_scale(which, recv):
        pltpu.make_async_copy(recv, recv, st_recv.at[which]).wait()
        stat_send[4 + which, 0:2, :] = stat_send[which, 0:2, :] + jnp.sum(recv[...], axis=0)
        total = all_groups(stat_send[4 + which], REG // 32)
        return scale_shift(
            total[0:1], total[1:2], float(BAND_ROWS * BAND_COLS * (REG // 32))
        )

    def send_patch(which, s, q, recv):
        s = jnp.sum(s, axis=0, keepdims=True)
        q = jnp.sum(q, axis=0, keepdims=True)
        stat_send[which, 0:1, :] = s[:, :128]
        stat_send[which, 1:2, :] = s[:, 128:]
        stat_send[which, 2:3, :] = q[:, :128]
        stat_send[which, 3:4, :] = q[:, 128:]
        for step in range(1, LAT):
            pltpu.make_async_remote_copy(
                src_ref=stat_send.at[which, pl.ds(0, 4)],
                dst_ref=recv.at[step - 1],
                send_sem=st_send.at[which],
                recv_sem=st_recv.at[which],
                device_id={"lat": lax.rem(lat + step, LAT)},
                device_id_type=MESH,
            ).start()

    def patch_scale(which, recv):
        pltpu.make_async_copy(recv, recv, st_recv.at[which]).wait()
        stat_send[4 + which, 0:4, :] = stat_send[which, 0:4, :] + jnp.sum(recv[...], axis=0)
        total = all_groups(stat_send[4 + which], DIF // 32)
        sums = jnp.concatenate([total[0:1], total[1:2]], axis=1)
        squares = jnp.concatenate([total[2:3], total[3:4]], axis=1)
        return scale_shift(sums, squares, float(BAND_ROWS * PATCH * (DIF // 32)))

    stats = [first_rows(1, 3, 6), first_rows(2, 2, 4), first_rows(3, 0, 3)]
    stat_send[...] = jnp.zeros_like(stat_send)
    send_band(0, sum(s for s, _ in stats), sum(q for _, q in stats), stat_one)

    put_window(0)
    put_window(4)
    first_rows(0, 0, 6)
    first_rows(1, 2, 3)
    first_rows(3, 3, 6)
    first_rows(4, 2, 6)
    own_xt = xt_far[OFF : OFF + PATCH, :256]
    put_part(1, own_xt)

    def patch_rows(win):
        return ((3, 6), (2, 4), (0, 3))[win]

    def rest_rows(win):
        return ((0, 3), None, (3, 6))[win]

    for win in range(3):
        for span in (patch_rows(win), rest_rows(win)):
            if span is None:
                continue
            low, high = span
            out = jnp.dot(
                parts[win, :, 0:768],
                wb_patch[0:768, low * DIF : high * DIF],
                preferred_element_type=F32,
            )
            for p in range(low, high):
                e = win * 4 + 5 + p
                partial[(e - 5) * PATCH : (e - 4) * PATCH, :] = out[
                    :, (p - low) * DIF : (p - low + 1) * DIF
                ]

    def activate_band(source, a, b, e):
        ok = row_ok(e)
        at = at_row(e, W)
        half = source[pl.ds(at, W), :].astype(F32) * (a * ok) + b * ok
        out = half_silu(half)
        act[0, pl.ds(at, W), :] = pltpu.roll(out, 1, axis=0).astype(BF16)
        act[1, pl.ds(at, W), :] = out.astype(BF16)
        act[2, pl.ds(at, W), :] = pltpu.roll(out, W - 1, axis=0).astype(BF16)

    def loop(count, body):
        lax.fori_loop(0, count, lambda i, c: (body(i), c)[1], 0)

    def conv_band(weight, e, pairs):
        def rows_of(q, dx):
            return [
                act[dx, pl.ds(at_row(e + 2 * k + q - 1, W), W), :] for k in range(pairs)
            ]

        lhs = jnp.concatenate(
            [
                jnp.concatenate(rows_of(q, dx), axis=0)
                for q in range(4)
                for dx in range(3)
            ],
            axis=1,
        )
        out = jnp.dot(lhs, weight[...], preferred_element_type=F32)
        return [
            out[(r // 2) * W : (r // 2 + 1) * W, (r % 2) * REG : (r % 2 + 1) * REG]
            for r in range(2 * pairs)
        ]

    a, b = band_scale(0, stat_one)
    for load in loads[0]:
        load.wait()
    s = jnp.zeros((8, REG), F32)
    q = jnp.zeros((8, REG), F32)
    ready = 7
    for e, pairs in SECOND_GROUPS:
        while ready <= e + 2 * pairs:
            activate_band(first, a, b, ready)
            ready += 1
        for i, out in enumerate(conv_band(w_one, e, pairs)):
            out = out.astype(BF16)
            second[(e + i) * W : (e + i + 1) * W, :] = out
            cell = out[SIDE : SIDE + COLS].astype(F32)
            s = s + fold(cell)
            q = q + fold(cell * cell)
    send_band(1, s, q, stat_two)

    def second_rest(i):
        e = 2 + i * 14
        for k, out in enumerate(conv_band(w_one, e, 3)):
            second[pl.ds(at_row(e + k, W), W), :] = out.astype(BF16)

    loop(12, lambda i: activate_band(first, a, b, 1 + i + (i // 6) * 10))
    loop(2, second_rest)

    a2, b2 = band_scale(1, stat_two)
    for load in loads[1]:
        load.wait()

    def third_rows(e, pairs):
        for k, out in enumerate(conv_band(w_two, e, pairs)):
            at = at_row(e + k, W)
            out = first[pl.ds(at, W), :].astype(F32) + out
            third[pl.ds(at, W), :] = (out * row_ok(e + k)).astype(BF16)

    ready = 5
    for e, pairs in THIRD_GROUPS:
        while ready <= e + 2 * pairs:
            activate_band(second, a2, b2, ready)
            ready += 1
        third_rows(e, pairs)

    def mean_windows(starts):
        lhs = jnp.concatenate(
            [
                jnp.concatenate([third[(e + i - 1) * W : (e + i) * W, :] for e in starts], axis=0)
                for i in range(6)
            ],
            axis=1,
        )
        out = jnp.dot(lhs, wb_mean[...], preferred_element_type=F32)
        windows = []
        for k, e in enumerate(starts):
            low, high = out[k * W : (k + 1) * W, 0:128], out[k * W : (k + 1) * W, 128:256]
            mean = (
                pltpu.roll(low, 1, axis=0)
                + pltpu.roll(low, 64, axis=1)
                + pltpu.roll(high, W - 1, axis=0)
            )
            ok = jnp.zeros((1, 128), F32)
            for q in range(4):
                ok = jnp.where(lane128 // CH == q, row_ok(e + q), ok)
            windows.append(mean[OFF : OFF + PATCH] * ok)
        return windows

    def put_mixed(windows):
        for k, mean in enumerate(windows):
            at = k * PATCH
            later = pltpu.roll(mean, 1, axis=0)
            sooner = pltpu.roll(mean, PATCH - 1, axis=0)
            low = jnp.where(half_lane, later, pltpu.roll(mean, 64, axis=1))
            head = jnp.where((spot_low == 0) & half_lane, 0.0, low[:16])
            tail = jnp.where(spot_low == 15, 0.0, sooner[-16:])
            mixed[at : at + 16, 0:128] = head.astype(BF16)
            mixed[at + 16 : at + PATCH, 0:128] = low[16:].astype(BF16)
            mixed[at : at + PATCH - 16, 128:256] = sooner[:-16].astype(BF16)
            mixed[at + PATCH - 16 : at + PATCH, 128:256] = tail.astype(BF16)

    def patch_first_rows(starts, skip):
        out = jnp.dot(mixed[...], wb_mix[...], preferred_element_type=F32)
        s = jnp.zeros((8, DIF), F32)
        q = jnp.zeros((8, DIF), F32)
        for k, start in enumerate(starts):
            for p in range(2):
                e = start + 1 + p
                if (k, p) in skip:
                    continue
                at = (e - 5) * PATCH
                row = out[k * PATCH : (k + 1) * PATCH, p * DIF : (p + 1) * DIF]
                row = (row + partial[at : at + PATCH, :]).astype(BF16)
                p_first[at : at + PATCH, :] = row
                if 8 <= e < 16:
                    cell = row.astype(F32)
                    s = s + fold(cell)
                    q = q + fold(cell * cell)
        return s, q

    windows = mean_windows((7, 9, 11, 13))
    put_mixed(windows)
    for k, mean in enumerate(windows):
        mean_keep[k] = mean
    s, q = patch_first_rows((7, 9, 11, 13), ())
    send_patch(2, s, q, stat_three)

    def activate_rest(i):
        activate_band(second, a2, b2, 2 + i + (i // 3) * 14)

    loop(6, activate_rest)
    loop(2, lambda i: third_rows(3 + 14 * i, 2))
    put_mixed(mean_windows((4, 6, 15, 16)))
    patch_first_rows((4, 6, 15, 16), ((1, 1), (3, 0)))
    mean_own = jnp.zeros((PATCH, 128), F32)
    for k in range(4):
        here = lane128 // 32 == k
        mean_own = jnp.where(here, pltpu.roll(mean_keep[k], (32 * k - CH) % 128, axis=1), mean_own)
    noise_own = pltpu.roll(noise_keep[...], 192, axis=1)[:, :128]
    base = mean_own + noise_own

    def put_out(out_ref, values):
        flat = pltpu.roll(values.T, PATCH - MARGIN, axis=1)[:, :COLS]
        for r in range(ROWS):
            out_ref[:, r, :] = flat[r * CH : r * CH + OUTC, :]

    put_out(mean_out, mean_own)
    pad32[...] = base

    spot16 = lax.broadcasted_iota(jnp.int32, (16, DIF), 0)

    def activate_patch(source, shift_row, a, b, e):
        ok = row_ok(e)
        half = source[pl.ds(at_row(e - shift_row, PATCH), PATCH), :].astype(F32) * (a * ok) + b * ok
        out = half_silu(half)
        at = at_row(e - 5, PATCH)
        later = pltpu.roll(out, 1, axis=0)
        sooner = pltpu.roll(out, PATCH - 1, axis=0)
        p_act[0, pl.ds(at, 16), :] = jnp.where(spot16 == 0, 0.0, later[:16]).astype(BF16)
        p_act[0, pl.ds(at + 16, PATCH - 16), :] = later[16:].astype(BF16)
        p_act[1, pl.ds(at, PATCH), :] = out.astype(BF16)
        p_act[2, pl.ds(at, PATCH - 16), :] = sooner[:-16].astype(BF16)
        p_act[2, pl.ds(at + PATCH - 16, 16), :] = jnp.where(
            spot16 == 15, 0.0, sooner[-16:]
        ).astype(BF16)

    def conv_patch(weight, e, rows):
        lhs = jnp.concatenate(
            [
                p_act[dx, pl.ds(at_row(e + dy - 6, PATCH), rows * PATCH), :]
                for dy in range(3)
                for dx in range(3)
            ],
            axis=1,
        )
        return jnp.dot(lhs, weight[...], preferred_element_type=F32)

    a3, b3 = patch_scale(2, stat_three)
    for load in loads[2]:
        load.wait()
    s = jnp.zeros((8, DIF), F32)
    q = jnp.zeros((8, DIF), F32)
    ready = 7
    for e, rows in P_SECOND_GROUPS:
        while ready <= e + rows:
            activate_patch(p_first, 5, a3, b3, ready)
            ready += 1
        out = conv_patch(d_one, e, rows).astype(BF16)
        p_second[(e - 6) * PATCH : (e - 6 + rows) * PATCH, :] = out
        cell = out.astype(F32)
        s = s + fold(cell)
        q = q + fold(cell * cell)
    send_patch(3, s, q, stat_four)

    def p_second_rest(i):
        e = 6 + i * 10
        out = conv_patch(d_one, e, 2).astype(BF16)
        p_second[pl.ds(at_row(e - 6, PATCH), 2 * PATCH), :] = out

    loop(4, lambda i: activate_patch(p_first, 5, a3, b3, 5 + i + (i // 2) * 10))
    loop(2, p_second_rest)

    a4, b4 = patch_scale(3, stat_four)
    for load in loads[3]:
        load.wait()
    ready = 6
    for e, rows in P_THIRD_GROUPS:
        while ready <= e + rows:
            activate_patch(p_second, 6, a4, b4, ready)
            ready += 1
        conv = conv_patch(d_two, e, rows)
        for k in range(rows):
            out = p_first[(e + k - 5) * PATCH : (e + k - 4) * PATCH, :].astype(F32)
            out = (out + conv[k * PATCH : (k + 1) * PATCH]) * row_ok(e + k)
            p_third[(e + k - 7) * PATCH : (e + k - 6) * PATCH, :] = out.astype(BF16)

    lhs = jnp.concatenate(
        [
            jnp.concatenate([p_third[r * PATCH : (r + 1) * PATCH, :] for r in (i, i + 4)], axis=0)
            for i in range(6)
        ],
        axis=1,
    )
    out = jnp.dot(lhs, wb_vel[...], preferred_element_type=F32)

    def of_window(k):
        low, high = out[k * PATCH : (k + 1) * PATCH, :128], out[k * PATCH : (k + 1) * PATCH, 128:]
        return shift(low, 0) + pltpu.roll(low, 64, axis=1) + shift(high, 2)

    velocity = jnp.where(half_lane, of_window(0), pltpu.roll(of_window(1), 64, axis=1))
    edge_send[0] = velocity[0:MARGIN]
    edge_send[1] = velocity[PATCH - MARGIN : PATCH]
    edges = [
        pltpu.make_async_remote_copy(
            src_ref=edge_send.at[k],
            dst_ref=edge_recv.at[k],
            send_sem=e_send.at[k],
            recv_sem=e_recv.at[k],
            device_id={"lon": lax.rem(lon + LON + step, LON)},
            device_id_type=MESH,
        )
        for k, step in ((0, -1), (1, 1))
    ]
    for edge in edges:
        edge.start()
    total = jnp.concatenate(
        [
            velocity[0:MARGIN],
            velocity[MARGIN : 2 * MARGIN] * 0.5,
            velocity[2 * MARGIN : COLS],
            velocity[COLS : COLS + MARGIN] * 0.5,
            velocity[COLS + MARGIN :],
        ],
        axis=0,
    )
    own32[...] = pltpu.roll((pad32[...] + total).T, PATCH - MARGIN, axis=1)
    for k in order:
        copies[k].wait_send()
    for which, recv in enumerate((stat_one, stat_two, stat_three, stat_four)):
        pltpu.make_async_copy(recv, recv, st_send.at[which]).wait()
    for edge in edges:
        edge.wait()
    margins = jnp.concatenate(
        [edge_recv[1], edge_recv[0], jnp.zeros((2 * MARGIN, 128), F32)], axis=0
    ).T
    margins = margins * 0.5
    left = jnp.where(lane128 < MARGIN, margins, 0.0)
    flat = own32[...] + jnp.concatenate([left, margins - left], axis=1)
    for r in range(ROWS):
        field_out[:, r, :] = flat[r * CH : r * CH + OUTC, :COLS]


def hand_over(mean_in, field_in, mean_out, field_out):
    mean_out[...] = mean_in[...]
    field_out[...] = field_in[...]


def on_device(coarse, static, noise_seeds, w_in, w_one, w_two, w_out, d_in, d_one, d_two, d_out):
    vmem = pl.BlockSpec(memory_space=pltpu.VMEM)
    smem = pl.BlockSpec(memory_space=pltpu.SMEM)
    hbm = pl.BlockSpec(memory_space=pl.ANY)
    out = jax.ShapeDtypeStruct((OUTC, ROWS, COLS), F32)
    results = pl.pallas_call(
        kernel,
        out_shape=(pltpu.VMEM((OUTC, ROWS, COLS), F32),) * 2,
        in_specs=[hbm, hbm, smem] + [hbm] * 8,
        out_specs=(vmem, vmem),
        scratch_shapes=[
            pltpu.VMEM((OUTC, ROWS, COLS), F32),
            pltpu.VMEM((CH - OUTC, ROWS, COLS), F32),
            pltpu.VMEM((9, CH, REG), BF16),
            pltpu.VMEM((9, OUTC, REG), BF16),
            pltpu.VMEM((9, 40, DIF), BF16),
            pltpu.VMEM((9, OUTC, DIF), BF16),
            pltpu.VMEM((12 * REG, 2 * REG), BF16),
            pltpu.VMEM((12 * REG, 2 * REG), BF16),
            pltpu.VMEM((9 * DIF, DIF), BF16),
            pltpu.VMEM((9 * DIF, DIF), BF16),
            pltpu.VMEM((128, 256), F32),
            pltpu.VMEM((128, 256), BF16),
            pltpu.VMEM((2, 128, 256), BF16),
            pltpu.VMEM((6, 128, 128), BF16),
            pltpu.VMEM((5, W, 384), BF16),
            pltpu.VMEM((384, 6 * REG), BF16),
            pltpu.VMEM((768, 6 * DIF), BF16),
            pltpu.VMEM((256, 2 * DIF), BF16),
            pltpu.VMEM((6 * REG, 256), BF16),
            pltpu.VMEM((6 * DIF, 256), BF16),
            pltpu.VMEM((FRAME * W, REG), BF16),
            pltpu.VMEM((FRAME * W, REG), BF16),
            pltpu.VMEM((FRAME * W, REG), BF16),
            pltpu.VMEM((3, FRAME * W, REG), BF16),
            pltpu.VMEM((PATCH, 256), F32),
            pltpu.VMEM((3, PATCH, 768), BF16),
            pltpu.VMEM((4 * PATCH, 256), BF16),
            pltpu.VMEM((14 * PATCH, DIF), F32),
            pltpu.VMEM((4, PATCH, 128), F32),
            pltpu.VMEM((14 * PATCH, DIF), BF16),
            pltpu.VMEM((12 * PATCH, DIF), BF16),
            pltpu.VMEM((10 * PATCH, DIF), BF16),
            pltpu.VMEM((3, 14 * PATCH, DIF), BF16),
            pltpu.VMEM((256, 128), F32),
            pltpu.VMEM((128, DIF), F32),
            pltpu.VMEM((2, MARGIN, 128), F32),
            pltpu.VMEM((2, MARGIN, 128), F32),
            pltpu.VMEM((8, 8, 128), F32),
            pltpu.VMEM((ALL - 1, 2, 128), F32),
            pltpu.VMEM((ALL - 1, 2, 128), F32),
            pltpu.VMEM((LAT - 1, 4, 128), F32),
            pltpu.VMEM((LAT - 1, 4, 128), F32),
            pltpu.SemaphoreType.DMA((12,)),
            pltpu.SemaphoreType.DMA((8,)),
            pltpu.SemaphoreType.DMA((8,)),
            pltpu.SemaphoreType.DMA((4,)),
            pltpu.SemaphoreType.DMA((4,)),
            pltpu.SemaphoreType.DMA((2,)),
            pltpu.SemaphoreType.DMA((2,)),
        ],
        compiler_params=pltpu.CompilerParams(
            collective_id=0, has_side_effects=True, vmem_limit_bytes=60 * 1024 * 1024
        ),
    )(
        coarse,
        static,
        noise_seeds,
        w_in.reshape(9, CH, REG),
        w_one.reshape(9 * REG, REG),
        w_two.reshape(9 * REG, REG),
        jnp.transpose(w_out.reshape(9, REG, OUTC), (0, 2, 1)),
        d_in.reshape(9, 40, DIF),
        d_one.reshape(9 * DIF, DIF),
        d_two.reshape(9 * DIF, DIF),
        jnp.transpose(d_out.reshape(9, DIF, OUTC), (0, 2, 1)),
    )
    return pl.pallas_call(
        hand_over,
        out_shape=(out, out),
        in_specs=[vmem, vmem],
        out_specs=(vmem, vmem),
        compiler_params=pltpu.CompilerParams(vmem_limit_bytes=4 * 1024 * 1024),
    )(*results)


def solution(mesh):
    brick = P(None, "lat", "lon")
    return jax.shard_map(
        on_device,
        mesh=mesh,
        in_specs=(brick, brick) + (P(),) * 9,
        out_specs=(brick, brick),
        check_vma=False,
    )
```
